256 devices in a mesh: ens: 4 (over y_hi, core), grid: 64 (over z, x, y_lo).
Axes of the slice: x: 4, y: 4 (y_hi: 2, y_lo: 2; y = y_hi * 2 + y_lo), z: 8, core: 2. Of those that a mesh axis runs over, the one named last changes fastest.
Arguments:
- grid_embed: bfloat16 [8, 8192, 1024], P('ens', 'grid'), may hold values from -6 to 6
- latent: bfloat16 [8, 2048, 1024], P('ens', 'grid'), may hold values from -6 to 6
- key_weight: bfloat16 [1024, 1024], replicated, may hold values from -0.1875 to 0.1875
- value_weight: bfloat16 [1024, 1024], replicated, may hold values from -0.1875 to 0.1875
- out_weight: bfloat16 [100, 1024], replicated, may hold values from -0.1875 to 0.1875
- target: float32 [100, 8192], P(None, 'grid'), may hold values from -6 to 6
- edges: int32 [2, 32768], P(None, 'grid'), may hold values from -1 to 8191, as said below
Outputs:
- grad_key_weight: float32 [1024, 1024], P('grid')
- grad_value_weight: float32 [1024, 1024], P('grid')
- grad_out_weight_t: float32 [1024, 100], P('grid')
- grad_latent: float32 [8, 2048, 1024], P('ens', 'grid')
The draws below stay inside these ranges and needn't reach their ends.
Inputs may be any that keep to these rules, and one draw needn't show every extreme that they name: The 512 slots of band s start at position s * 512: its live edges come first, then padding. A live edge's destination is a grid point of band s (s * 128 to (s + 1) * 128 - 1) and its source a latent node of bands s and s + 1 (s * 32 to (s + 2) * 32 - 1; only band s's own on the last band). Padding has destination -1 and source s * 32. Every grid point is the destination of 1 to 4 edges; in some bands every slot is live.
All inputs are finite; a program needn't handle non-finite values.
Results may differ from the reference program's by a relative error of at most 0.017.
Values may be sent and summed in bfloat16 or wider, within the bound.
No kernel may reach another device: no remote copies, remote signals or barrier semaphores. Data moves between devices by JAX's collectives and lax.ppermute only.
A program may use at most 128 MiB of HBM per device.

```python
import jax
import jax.numpy as jnp
from jax import lax

D = 1024
HEADS = 16
HEAD_DIM = 64
VARS = 100
GRID_DEV = 128
LAT_DEV = 32
MEMBERS = 8
GRID = 8192
LATENT = 2048
EDGE_DEV = 512
N_GRID = 64


def draw_edges(key, part):
    key = jax.random.fold_in(key, 11)
    key_degree = jax.random.fold_in(key, 1)
    key_source = jax.random.fold_in(key, 2)
    band = jnp.arange(N_GRID, dtype=jnp.int32)[:, None, None]
    polar = (band == 0) | (band == N_GRID - 1)
    degree = jax.random.randint(key_degree, (N_GRID, GRID_DEV, 1), 1, 4, dtype=jnp.int32)
    degree = jnp.where(polar, 4, degree)
    slot = jnp.arange(4, dtype=jnp.int32)[None, None, :]
    valid = slot < degree
    row_index = jnp.arange(GRID_DEV, dtype=jnp.int32)[None, :, None]
    dst_all = jnp.where(valid, band * GRID_DEV + row_index, -1).reshape(N_GRID, 4 * GRID_DEV)
    offset = jax.random.randint(key_source, (N_GRID, GRID_DEV, 4), 0, 2 * LAT_DEV, dtype=jnp.int32)
    offset = jnp.where(band < N_GRID - 1, offset, offset % LAT_DEV)
    src_all = jnp.where(valid, band * LAT_DEV + offset, band * LAT_DEV).reshape(N_GRID, 4 * GRID_DEV)
    order = jnp.argsort(jnp.where(dst_all >= 0, 0, 1).astype(jnp.int32), axis=1, stable=True)
    dst_all = jnp.take_along_axis(dst_all, order, axis=1)
    src_all = jnp.take_along_axis(src_all, order, axis=1)
    return jnp.stack([dst_all.reshape(-1), src_all.reshape(-1)]).astype(jnp.int32)


def level_of(key, extent, cuts, low, top_value):
    loudness = 1.0
    for dim, shards_of in cuts:
        draws = jax.random.uniform(jax.random.fold_in(jax.random.fold_in(key, 6), dim), (shards_of,), jnp.float32, low / len(cuts), top_value / len(cuts))
        loudness = loudness * jnp.repeat(jnp.exp(draws), extent[dim] // shards_of).reshape((-1,) + (1,) * (len(extent) - 1 - dim))
    return loudness


def normal_values(own_key, shape, deviation, most, shards=(), kind=jnp.bfloat16):
    drawn = deviation * jax.random.normal(own_key, shape, jnp.float32)
    if shards:
        drawn = drawn * level_of(own_key, shape, shards, -0.22, 0.18)
    return jnp.clip(drawn, -most, most).astype(kind)


def setup_inputs(seed: int = 0) -> dict:
    seeds = jax.random.split(jax.random.key(seed), 8)
    return {
        "grid_embed": normal_values(seeds[0], (MEMBERS, GRID, D), 1.0, 6.0, ((0, 4), (1, 64))),
        "latent": normal_values(seeds[1], (MEMBERS, LATENT, D), 1.0, 6.0, ((0, 4), (1, 64))),
        "key_weight": normal_values(seeds[2], (D, D), D ** -0.5, 0.1875),
        "value_weight": normal_values(seeds[3], (D, D), D ** -0.5, 0.1875),
        "out_weight": normal_values(seeds[4], (VARS, D), D ** -0.5, 0.1875),
        "target": normal_values(seeds[5], (VARS, GRID), 1.0, 6.0, ((1, 64),), jnp.float32),
        "edges": draw_edges(jax.random.fold_in(seeds[7], 71), 0),
    }


CAP = 5.0
DELTA_SQ = 0.0625
EPS = 1e-06

def slope(offset):
    return offset / jnp.sqrt(offset * offset + DELTA_SQ)

def project(rows, weight):
    return jnp.dot(rows, weight, preferred_element_type=jnp.float32).astype(jnp.bfloat16)

def edge_rows(queries, key_rows, value_rows, targets, sources):
    valid = targets >= 0
    target_rows = jnp.where(valid, targets, 0)
    query_edge = jnp.take(queries, target_rows, axis=0).astype(jnp.float32).reshape(-1, HEADS, HEAD_DIM)
    key_edge = jnp.take(key_rows, sources, axis=0).astype(jnp.float32).reshape(-1, HEADS, HEAD_DIM)
    value_edge = jnp.take(value_rows, sources, axis=0).astype(jnp.float32).reshape(-1, HEADS, HEAD_DIM)
    return (valid, target_rows, query_edge, key_edge, value_edge)

def attend_forward(queries, key_rows, value_rows, targets, sources):
    valid, target_rows, query_edge, key_edge, value_edge = edge_rows(queries, key_rows, value_rows, targets, sources)
    grid_count = queries.shape[0]
    raw_scores = lax.optimization_barrier(jnp.sum(query_edge * key_edge, axis=-1)) * HEAD_DIM ** (-0.5)
    capped = CAP * jnp.tanh(raw_scores / CAP)
    exp_scores = jnp.where(valid[:, None], jnp.exp(capped), 0.0)
    totals = jax.ops.segment_sum(exp_scores, target_rows, num_segments=grid_count)
    weights = exp_scores / jnp.take(totals, target_rows, axis=0)
    attended = jax.ops.segment_sum(weights[:, :, None] * value_edge, target_rows, num_segments=grid_count)
    return (attended, weights, capped)

def attend_backward(attn_grad, attended, weights, capped, queries, key_rows, value_rows, targets, sources):
    valid, target_rows, query_edge, key_edge, value_edge = edge_rows(queries, key_rows, value_rows, targets, sources)
    row_count = key_rows.shape[0]
    edge_grad = jnp.take(attn_grad, target_rows, axis=0)
    weight_grad = lax.optimization_barrier(jnp.sum(edge_grad * value_edge, axis=-1))
    inner = lax.optimization_barrier(jnp.sum(attn_grad * attended, axis=-1))
    capped_grad = weights * (weight_grad - jnp.take(inner, target_rows, axis=0))
    raw_grad = capped_grad * (1.0 - capped / CAP * (capped / CAP)) * HEAD_DIM ** (-0.5)
    key_edge_grad = (raw_grad[:, :, None] * query_edge).reshape(-1, D)
    value_edge_grad = (weights[:, :, None] * edge_grad).reshape(-1, D)
    key_part = jax.ops.segment_sum(key_edge_grad, sources, num_segments=row_count)
    value_part = jax.ops.segment_sum(value_edge_grad, sources, num_segments=row_count)
    return (key_part, value_part)

def reference(grid_embed, latent, key_weight, value_weight, out_weight, target, edges):
    band_ids = jnp.arange(N_GRID, dtype=jnp.int32)
    member_ids = jnp.arange(MEMBERS, dtype=jnp.int32)
    dst_bands = edges[0].reshape(N_GRID, EDGE_DEV)
    src_bands = edges[1].reshape(N_GRID, EDGE_DEV)
    padding = jnp.zeros((LAT_DEV, D), jnp.bfloat16)

    def band_inputs(member_embed, key_ext, value_ext, index):
        start = index * GRID_DEV
        queries = lax.dynamic_slice_in_dim(member_embed, start, GRID_DEV, 0)
        window_keys = lax.dynamic_slice_in_dim(key_ext, index * LAT_DEV, 2 * LAT_DEV, 0)
        window_values = lax.dynamic_slice_in_dim(value_ext, index * LAT_DEV, 2 * LAT_DEV, 0)
        dst_row = dst_bands[index]
        targets = jnp.where(dst_row >= 0, dst_row - start, -1).astype(jnp.int32)
        sources = (src_bands[index] - index * LAT_DEV).astype(jnp.int32)
        return (queries, window_keys, window_values, targets, sources)

    def member_forward(member):
        member_embed = grid_embed[member]
        key_ext = jnp.concatenate([project(latent[member], key_weight), padding], axis=0)
        value_ext = jnp.concatenate([project(latent[member], value_weight), padding], axis=0)

        def band_forward(index):
            queries, window_keys, window_values, targets, sources = band_inputs(member_embed, key_ext, value_ext, index)
            return attend_forward(queries, window_keys, window_values, targets, sources)[0].reshape(GRID_DEV, D)
        attended = lax.map(band_forward, band_ids).reshape(GRID, D)
        mixed = member_embed.astype(jnp.float32) + attended
        inverse = lax.rsqrt(lax.optimization_barrier(jnp.mean(mixed * mixed, axis=-1, keepdims=True)) + EPS)
        normed = mixed * inverse
        prediction = lax.dot_general(out_weight, normed.astype(jnp.bfloat16), (((1,), (1,)), ((), ())), preferred_element_type=jnp.float32)
        return (prediction, normed, inverse, key_ext, value_ext)

    def member_prediction(member):
        return member_forward(member)[0]
    preds = lax.map(member_prediction, member_ids)

    def member_backward(carry, member):
        prediction, normed, inverse, key_ext, value_ext = member_forward(member)
        member_embed = grid_embed[member]
        pair_term = lax.optimization_barrier(jnp.sum(slope(prediction[None] - preds), axis=0))
        pred_grad = (slope(prediction - target) / MEMBERS - pair_term / (MEMBERS * (MEMBERS - 1))).astype(jnp.bfloat16)
        normed_low = normed.astype(jnp.bfloat16)
        out_grad = lax.dot_general(normed_low, pred_grad, (((0,), (1,)), ((), ())), preferred_element_type=jnp.float32)
        normed_grad = lax.dot_general(pred_grad, out_weight, (((0,), (0,)), ((), ())), preferred_element_type=jnp.float32)
        mixed_grad = inverse * (normed_grad - normed * lax.optimization_barrier(jnp.mean(normed_grad * normed, axis=-1, keepdims=True)))

        def band_backward(grads, index):
            queries, window_keys, window_values, targets, sources = band_inputs(member_embed, key_ext, value_ext, index)
            attended, weights, capped = attend_forward(queries, window_keys, window_values, targets, sources)
            band_grad = lax.dynamic_slice_in_dim(mixed_grad, index * GRID_DEV, GRID_DEV, 0).reshape(GRID_DEV, HEADS, HEAD_DIM)
            key_part, value_part = attend_backward(band_grad, attended, weights, capped, queries, window_keys, window_values, targets, sources)
            start = index * LAT_DEV
            key_acc = lax.dynamic_update_slice_in_dim(grads[0], lax.dynamic_slice_in_dim(grads[0], start, 2 * LAT_DEV, 0) + key_part, start, 0)
            value_acc = lax.dynamic_update_slice_in_dim(grads[1], lax.dynamic_slice_in_dim(grads[1], start, 2 * LAT_DEV, 0) + value_part, start, 0)
            return ((key_acc, value_acc), None)
        zero_grads = jnp.zeros((LATENT + LAT_DEV, D), jnp.float32)
        accum, unused = lax.scan(band_backward, (zero_grads, zero_grads), band_ids)
        key_grad = accum[0][:LATENT].astype(jnp.bfloat16)
        value_grad = accum[1][:LATENT].astype(jnp.bfloat16)
        member_latent = latent[member]
        key_weight_grad = lax.dot_general(member_latent, key_grad, (((0,), (0,)), ((), ())), preferred_element_type=jnp.float32)
        value_weight_grad = lax.dot_general(member_latent, value_grad, (((0,), (0,)), ((), ())), preferred_element_type=jnp.float32)
        latent_grad = jnp.dot(key_grad, key_weight.T, preferred_element_type=jnp.float32) + jnp.dot(value_grad, value_weight.T, preferred_element_type=jnp.float32)
        return ((carry[0] + key_weight_grad, carry[1] + value_weight_grad, carry[2] + out_grad), latent_grad)
    start_carry = (jnp.zeros((D, D), jnp.float32), jnp.zeros((D, D), jnp.float32), jnp.zeros((D, VARS), jnp.float32))
    totals, grad_latent = lax.scan(member_backward, start_carry, member_ids)
    return (totals[0], totals[1], totals[2], grad_latent)
```

```python
import jax
import jax.numpy as jnp
from jax import lax
from jax.experimental import pallas as pl
from jax.experimental.pallas import tpu as pltpu
from jax.sharding import Mesh
from jax.sharding import PartitionSpec as P

HEAD_DIM = 64
CAP = 5.0
DELTA_SQ = 0.0625
EPS = 1e-06

MEMBERS = 8
HELD = 2
GRID_DEV = 128
LAT_DEV = 32
WINDOW = 64
D = 1024
VARS = 100
VARS_PAD = 128
GROUP = 256
GROUPS = D // GROUP
BAND = ("z", "x", "y")
SPLIT = ("ens", "x")
REST = ("z", "y")
PEERS = 16
COLS = 2 * D // PEERS

F32 = jnp.float32
LOW = jnp.bfloat16


def slope(offset):
    return offset * lax.rsqrt(offset * offset + DELTA_SQ)


def dot(a, b, a_dim, b_dim):
    return lax.dot_general(a, b, (((a_dim,), (b_dim,)), ((), ())), preferred_element_type=F32)


def same_head():
    rows = lax.broadcasted_iota(jnp.int32, (GROUP, GROUP), 0) // HEAD_DIM
    cols = lax.broadcasted_iota(jnp.int32, (GROUP, GROUP), 1) // HEAD_DIM
    return rows == cols


def by_head(rows, same):
    return jnp.where(same, jnp.concatenate([rows] * 4, axis=0), jnp.zeros((), LOW))


def from_head(blocks):
    head = lax.broadcasted_iota(jnp.int32, (WINDOW, GROUP), 1) // HEAD_DIM
    total = blocks[:WINDOW]
    for h in range(1, 4):
        total = jnp.where(head == h, blocks[h * WINDOW : (h + 1) * WINDOW], total)
    return total


def forward_kernel(
    embed, lat_own, lat_up, key_weight, value_weight, out_weight, edges,
    preds, preds_low, normed_low, inverse, exps, damps, values, keys, mixed,
):
    rows = jnp.concatenate([lat_own[0], lat_up[0], lat_own[1], lat_up[1]], axis=0)
    keys[...] = dot(rows, key_weight[...], 1, 0).astype(LOW)
    values[...] = dot(rows, value_weight[...], 1, 0).astype(LOW)
    target = edges[0:1, :]
    local = jnp.where(target >= 0, target & (GRID_DEV - 1), -1)
    source = edges[1:2, :] - (target >> 7) * LAT_DEV
    slots = edges.shape[1]
    into = (lax.broadcasted_iota(jnp.int32, (GRID_DEV, slots), 0) == local).astype(F32).astype(LOW)
    node = lax.broadcasted_iota(jnp.int32, (GROUP, slots), 0) & (WINDOW - 1)
    out_of = (node == source).astype(F32).astype(LOW)
    count = dot(into, out_of, 1, 1)
    same = same_head()
    ones = same.astype(F32).astype(LOW)
    for m in range(HELD):
        square = jnp.zeros((GRID_DEV, 1), F32)
        for j in range(GROUPS):
            cols = slice(j * GROUP, (j + 1) * GROUP)
            query = embed[m, :, cols]
            key = by_head(keys[m * WINDOW : (m + 1) * WINDOW, cols], same)
            value = by_head(values[m * WINDOW : (m + 1) * WINDOW, cols], same)
            bent = jnp.tanh(dot(query, key, 1, 1) * (HEAD_DIM**-0.5 / CAP))
            exp = (count * jnp.exp(CAP * bent)).astype(LOW)
            exps[m, :, cols] = exp
            damps[m, :, cols] = ((1.0 - bent * bent) * HEAD_DIM**-0.5).astype(LOW)
            attended = dot(exp, value, 1, 0) / dot(exp, ones, 1, 0)
            sums = query.astype(F32) + attended
            mixed[:, cols] = sums
            square = square + jnp.sum(sums * sums, axis=1, keepdims=True)
        inv = lax.rsqrt(square * (1.0 / D) + EPS)
        low = (mixed[...] * inv).astype(LOW)
        normed_low[m] = low
        inverse[m] = jnp.broadcast_to(inv, (GRID_DEV, 128))
        pred = dot(out_weight[...], low, 1, 1)
        preds[m] = pred
        preds_low[m] = pred.astype(LOW)


def backward_kernel(
    embed, out_weight, target, preds, every, normed_low, inverse, exps, damps, values,
    own, upper, out_grad, grad,
):
    same = same_head()
    ones = same.astype(F32).astype(LOW)
    pred_grads = []
    for m in range(HELD):
        pred = preds[m]
        pair = jnp.zeros((VARS_PAD, GRID_DEV), F32)
        for e in range(MEMBERS // HELD):
            for k in range(HELD):
                pair = pair + slope(pred - every[e, k].astype(F32))
        for k in range(HELD):
            pair = pair - slope(pred - preds[k].astype(LOW).astype(F32))
            if k != m:
                pair = pair + slope(pred - preds[k])
        base = slope(pred - target[...]) * (1.0 / MEMBERS)
        pred_grads.append((base - pair * (1.0 / (MEMBERS * (MEMBERS - 1)))).astype(LOW))
    both = jnp.concatenate(pred_grads, axis=1)
    lows = jnp.concatenate([normed_low[0], normed_low[1]], axis=0)
    out_grad[...] = jnp.transpose(dot(both, lows, 1, 0)).astype(LOW)
    for m in range(HELD):
        slant = jnp.zeros((GRID_DEV, 1), F32)
        for j in range(GROUPS):
            cols = slice(j * GROUP, (j + 1) * GROUP)
            part = dot(pred_grads[m], out_weight[:, cols], 0, 0)
            grad[:, cols] = part
            slant = slant + jnp.sum(part * normed_low[m, :, cols].astype(F32), axis=1, keepdims=True)
        slant = slant * (1.0 / D)
        inv = inverse[m][:, :1]
        for j in range(GROUPS):
            cols = slice(j * GROUP, (j + 1) * GROUP)
            mixed_grad = (inv * (grad[:, cols] - normed_low[m, :, cols].astype(F32) * slant)).astype(LOW)
            value = by_head(values[m * WINDOW : (m + 1) * WINDOW, cols], same)
            exp = exps[m, :, cols]
            weight = exp.astype(F32) / dot(exp, ones, 1, 0)
            weight_grad = dot(mixed_grad, value, 1, 1)
            term = weight * weight_grad
            high = term.astype(LOW)
            rest = (term - high.astype(F32)).astype(LOW)
            inner = dot(high, ones, 1, 0) + dot(rest, ones, 1, 0)
            raw_grad = (weight * (weight_grad - inner) * damps[m, :, cols].astype(F32)).astype(LOW)
            key_part = from_head(dot(raw_grad, embed[m, :, cols], 0, 0))
            value_part = from_head(dot(weight.astype(LOW), mixed_grad, 0, 0))
            own[0, m, :, cols] = key_part[:LAT_DEV]
            own[1, m, :, cols] = value_part[:LAT_DEV]
            upper[0, m, :, cols] = key_part[LAT_DEV:].astype(LOW)
            upper[1, m, :, cols] = value_part[LAT_DEV:].astype(LOW)


def join_kernel(own, lower, send):
    for which in range(2):
        for m in range(HELD):
            total = (own[which, m] + lower[which, m].astype(F32)).astype(LOW)
            for p in range(PEERS // 2):
                send[which * (PEERS // 2) + p, m * LAT_DEV : (m + 1) * LAT_DEV, :] = total[
                    :, p * COLS : (p + 1) * COLS
                ]


def latent_kernel(joined, key_weight, value_weight, grad_latent):
    half = PEERS // 2
    key_grad = jnp.concatenate([joined[p] for p in range(half)], axis=1)
    value_grad = jnp.concatenate([joined[half + p] for p in range(half)], axis=1)
    total = dot(key_grad, key_weight[...], 1, 1) + dot(value_grad, value_weight[...], 1, 1)
    for m in range(HELD):
        grad_latent[m] = total[m * LAT_DEV : (m + 1) * LAT_DEV]


def weight_kernel(parts, nodes, out_grad, send):
    rows = jnp.concatenate([parts[p] for p in range(PEERS)], axis=0)
    product = jnp.transpose(dot(rows, nodes[...], 0, 0)).astype(LOW)
    for z in range(8):
        for x in range(4):
            for y in range(2):
                start = ((z * 4 + x) * 2 + y) * 16
                send[z * 2 + y, x * 16 : (x + 1) * 16, :COLS] = product[start : start + 16]
                send[z * 2 + y, x * 16 : (x + 1) * 16, COLS:] = out_grad[start : start + 16]


def sum_kernel(parts, send):
    total = parts[0].astype(F32)
    for p in range(1, PEERS):
        total = total + parts[p].astype(F32)
    total = total.astype(LOW)
    for e in range(4):
        for x in range(4):
            send[e * 4 + x] = total[x * 16 : (x + 1) * 16]


def finish_kernel(parts, key_weight_grad, value_weight_grad, out_weight_grad):
    half = PEERS // 2
    total = parts[0, :, COLS:].astype(F32)
    for p in range(1, PEERS):
        total = total + parts[p, :, COLS:].astype(F32)
    out_weight_grad[...] = total[:, :VARS]
    for p in range(half):
        key_weight_grad[:, p * COLS : (p + 1) * COLS] = parts[p, :, :COLS].astype(F32)
        value_weight_grad[:, p * COLS : (p + 1) * COLS] = parts[half + p, :, :COLS].astype(F32)


def call(kernel, outs, scratch=(), flops=10**8, bytes_accessed=4 * 10**6):
    def run(*operands):
        return pl.pallas_call(
            kernel,
            out_shape=[jax.ShapeDtypeStruct(shape, kind) for shape, kind in outs],
            scratch_shapes=[pltpu.VMEM(shape, kind) for shape, kind in scratch],
            compiler_params=pltpu.CompilerParams(vmem_limit_bytes=48 * 2**20),
            cost_estimate=pl.CostEstimate(
                flops=flops, bytes_accessed=bytes_accessed, transcendentals=0
            ),
            name=kernel.__name__,
        )(*operands)

    return run


def band_shift(value, by):
    return lax.ppermute(value, BAND, [(i, i + by) for i in range(64) if 0 <= i + by < 64])


def on_device(grid_embed, latent, key_weight, value_weight, out_weight, target, edges):
    out_rows = jnp.pad(out_weight, ((0, VARS_PAD - VARS), (0, 0)))
    target = jnp.pad(target, ((0, VARS_PAD - VARS), (0, 0)))
    nodes = lax.all_gather(latent.reshape(HELD * LAT_DEV, D), SPLIT, axis=0, tiled=True)
    upper_latent = band_shift(latent, -1)
    preds, preds_low, normed_low, inverse, exps, damps, values = call(
        forward_kernel,
        [
            ((HELD, VARS_PAD, GRID_DEV), F32),
            ((HELD, VARS_PAD, GRID_DEV), LOW),
            ((HELD, GRID_DEV, D), LOW),
            ((HELD, GRID_DEV, 128), F32),
            ((HELD, GRID_DEV, D), LOW),
            ((HELD, GRID_DEV, D), LOW),
            ((HELD * WINDOW, D), LOW),
        ],
        [((HELD * WINDOW, D), LOW), ((GRID_DEV, D), F32)],
    )(grid_embed, latent, upper_latent, key_weight, value_weight, out_rows, edges)
    every = lax.all_gather(preds_low, "ens", axis=0)
    own, upper, out_grad = call(
        backward_kernel,
        [
            ((2, HELD, LAT_DEV, D), F32),
            ((2, HELD, LAT_DEV, D), LOW),
            ((D, VARS_PAD), LOW),
        ],
        [((GRID_DEV, D), F32)],
    )(grid_embed, out_rows, target, preds, every, normed_low, inverse, exps, damps, values)
    lower = band_shift(upper, 1)
    (joined,) = call(join_kernel, [((PEERS, HELD * LAT_DEV, COLS), LOW)])(own, lower)
    (grad_latent,) = call(latent_kernel, [((HELD, LAT_DEV, D), F32)])(
        joined, key_weight, value_weight
    )
    parts = lax.all_to_all(joined, SPLIT, 0, 0, tiled=True)
    (send,) = call(weight_kernel, [((PEERS, 64, 2 * COLS), LOW)])(parts, nodes, out_grad)
    parts = lax.all_to_all(send, REST, 0, 0, tiled=True)
    (send,) = call(sum_kernel, [((PEERS, 16, 2 * COLS), LOW)])(parts)
    parts = lax.all_to_all(send, SPLIT, 0, 0, tiled=True)
    results = call(finish_kernel, [((16, D), F32), ((16, D), F32), ((16, VARS), F32)])(parts)
    return (results[0], results[1], results[2], grad_latent)


def solution(mesh):
    wide = Mesh(mesh.devices.reshape(4, 8, 4, 2), ("ens", "z", "x", "y"))
    in_specs = (
        P("ens", BAND, None),
        P("ens", BAND, None),
        P(),
        P(),
        P(),
        P(None, BAND),
        P(None, BAND),
    )
    out_specs = (P(BAND, None), P(BAND, None), P(BAND, None), P("ens", BAND, None))
    return jax.shard_map(
        on_device, mesh=wide, in_specs=in_specs, out_specs=out_specs, check_vma=False
    )
```

```python
import jax
import jax.numpy as jnp
from jax import lax
from jax.experimental import pallas as pl
from jax.experimental.pallas import tpu as pltpu
from jax.sharding import Mesh
from jax.sharding import PartitionSpec as P

HEAD_DIM = 64
CAP = 5.0
DELTA_SQ = 0.0625
EPS = 1e-06

MEMBERS = 8
HELD = 2
GRID_DEV = 128
LAT_DEV = 32
WINDOW = 64
D = 1024
VARS = 100
VARS_PAD = 128
GROUP = 256
GROUPS = D // GROUP
BAND = ("z", "x", "y")
ENS = 4
PLANE = 8
SHARE = 16
COLS = 2 * D // ENS
PRED_ROW = 2 * LAT_DEV * GROUPS

F32 = jnp.float32
LOW = jnp.bfloat16


def slope(offset):
    return offset * lax.rsqrt(offset * offset + DELTA_SQ)


def dot(a, b, a_dim, b_dim):
    return lax.dot_general(a, b, (((a_dim,), (b_dim,)), ((), ())), preferred_element_type=F32)


def same_head():
    rows = lax.broadcasted_iota(jnp.int32, (GROUP, GROUP), 0) // HEAD_DIM
    cols = lax.broadcasted_iota(jnp.int32, (GROUP, GROUP), 1) // HEAD_DIM
    return rows == cols


def by_head(rows, same):
    return jnp.where(same, jnp.concatenate([rows] * 4, axis=0), jnp.zeros((), LOW))


def from_head(blocks):
    head = lax.broadcasted_iota(jnp.int32, (WINDOW, GROUP), 1) // HEAD_DIM
    total = blocks[:WINDOW]
    for h in range(1, 4):
        total = jnp.where(head == h, blocks[h * WINDOW : (h + 1) * WINDOW], total)
    return total


def own_kernel(latent, key_weight, value_weight, edges, keys, values, count):
    rows = jnp.concatenate([latent[0], latent[1]], axis=0)
    keys[...] = dot(rows, key_weight[...], 1, 0).astype(LOW)
    values[...] = dot(rows, value_weight[...], 1, 0).astype(LOW)
    target = edges[0:1, :]
    local = jnp.where(target >= 0, target & (GRID_DEV - 1), -1)
    source = edges[1:2, :] - (target >> 7) * LAT_DEV
    slots = edges.shape[1]
    into = (lax.broadcasted_iota(jnp.int32, (GRID_DEV, slots), 0) == local).astype(F32).astype(LOW)
    node = lax.broadcasted_iota(jnp.int32, (GROUP, slots), 0) & (WINDOW - 1)
    out_of = (node == source).astype(F32).astype(LOW)
    count[...] = dot(into, out_of, 1, 1)


def forward_kernel(
    embed, latent, lat_up, key_weight, value_weight, out_weight, own_keys, own_values, edge_count,
    preds, share, normed_low, inverse, exps, damps, values,
    keys, mixed,
):
    rows = jnp.concatenate([lat_up[0], lat_up[1]], axis=0)
    for own_rows, weight, window in ((own_keys, key_weight, keys), (own_values, value_weight, values)):
        upper_rows = dot(rows, weight[...], 1, 0).astype(LOW)
        for m in range(HELD):
            window[m * WINDOW : m * WINDOW + LAT_DEV] = own_rows[m * LAT_DEV : (m + 1) * LAT_DEV]
            window[m * WINDOW + LAT_DEV : (m + 1) * WINDOW] = upper_rows[m * LAT_DEV : (m + 1) * LAT_DEV]
    count = edge_count[...]
    same = same_head()
    ones = same.astype(F32).astype(LOW)
    for m in range(HELD):
        square = jnp.zeros((GRID_DEV, 1), F32)
        for j in range(GROUPS):
            cols = slice(j * GROUP, (j + 1) * GROUP)
            start = j * HELD * LAT_DEV + m * LAT_DEV
            share[start : start + LAT_DEV] = latent[m, :, cols]
            query = embed[m, :, cols]
            key = by_head(keys[m * WINDOW : (m + 1) * WINDOW, cols], same)
            value = by_head(values[m * WINDOW : (m + 1) * WINDOW, cols], same)
            bent = jnp.tanh(dot(query, key, 1, 1) * (HEAD_DIM**-0.5 / CAP))
            exp = (count * jnp.exp(CAP * bent)).astype(LOW)
            exps[m, :, cols] = exp
            damps[m, :, cols] = ((1.0 - bent * bent) * HEAD_DIM**-0.5).astype(LOW)
            attended = dot(exp, value, 1, 0) / dot(exp, ones, 1, 0)
            sums = query.astype(F32) + attended
            mixed[:, cols] = sums
            square = square + jnp.sum(sums * sums, axis=1, keepdims=True)
        inv = lax.rsqrt(square * (1.0 / D) + EPS)
        low = (mixed[...] * inv).astype(LOW)
        normed_low[m] = low
        inverse[m] = jnp.broadcast_to(inv, (GRID_DEV, 128))
        pred = dot(out_weight[...], low, 1, 1)
        preds[m] = pred
        share[PRED_ROW:, m * GRID_DEV : (m + 1) * GRID_DEV] = pred.astype(LOW)


def backward_kernel(
    embed, out_weight, target, preds, every, normed_low, inverse, exps, damps, values,
    own, upper, out_grad,
    grad, truth,
):
    truth[...] = jnp.zeros((VARS_PAD, GRID_DEV), F32)
    truth[:VARS, :] = target[...]
    same = same_head()
    ones = same.astype(F32).astype(LOW)
    pred_grads = []
    for m in range(HELD):
        pred = preds[m]
        pair = jnp.zeros((VARS_PAD, GRID_DEV), F32)
        for e in range(MEMBERS // HELD):
            for k in range(HELD):
                pair = pair + slope(pred - every[e, :, k * GRID_DEV : (k + 1) * GRID_DEV].astype(F32))
        for k in range(HELD):
            pair = pair - slope(pred - preds[k].astype(LOW).astype(F32))
            if k != m:
                pair = pair + slope(pred - preds[k])
        base = slope(pred - truth[...]) * (1.0 / MEMBERS)
        pred_grads.append((base - pair * (1.0 / (MEMBERS * (MEMBERS - 1)))).astype(LOW))
    both = jnp.concatenate(pred_grads, axis=1)
    lows = jnp.concatenate([normed_low[0], normed_low[1]], axis=0)
    out_grad[...] = jnp.transpose(dot(both, lows, 1, 0)).astype(LOW)
    for m in range(HELD):
        slant = jnp.zeros((GRID_DEV, 1), F32)
        for j in range(GROUPS):
            cols = slice(j * GROUP, (j + 1) * GROUP)
            part = dot(pred_grads[m], out_weight[:, cols], 0, 0)
            grad[:, cols] = part
            slant = slant + jnp.sum(part * normed_low[m, :, cols].astype(F32), axis=1, keepdims=True)
        slant = slant * (1.0 / D)
        inv = inverse[m][:, :1]
        for j in range(GROUPS):
            cols = slice(j * GROUP, (j + 1) * GROUP)
            mixed_grad = (inv * (grad[:, cols] - normed_low[m, :, cols].astype(F32) * slant)).astype(LOW)
            value = by_head(values[m * WINDOW : (m + 1) * WINDOW, cols], same)
            exp = exps[m, :, cols]
            weight = exp.astype(F32) / dot(exp, ones, 1, 0)
            weight_grad = dot(mixed_grad, value, 1, 1)
            term = weight * weight_grad
            high = term.astype(LOW)
            rest = (term - high.astype(F32)).astype(LOW)
            inner = dot(high, ones, 1, 0) + dot(rest, ones, 1, 0)
            raw_grad = (weight * (weight_grad - inner) * damps[m, :, cols].astype(F32)).astype(LOW)
            key_part = from_head(dot(raw_grad, embed[m, :, cols], 0, 0))
            value_part = from_head(dot(weight.astype(LOW), mixed_grad, 0, 0))
            own[0, m, :, cols] = key_part[:LAT_DEV]
            own[1, m, :, cols] = value_part[:LAT_DEV]
            upper[0, m, :, cols] = key_part[LAT_DEV:].astype(LOW)
            upper[1, m, :, cols] = value_part[LAT_DEV:].astype(LOW)


def join_kernel(own, lower, send):
    for which in range(2):
        for m in range(HELD):
            total = (own[which, m] + lower[which, m].astype(F32)).astype(LOW)
            for p in range(2):
                send[2 * which + p, m * LAT_DEV : (m + 1) * LAT_DEV, :] = total[
                    :, p * COLS : (p + 1) * COLS
                ]


def latent_kernel(joined, key_weight, value_weight, grad_latent):
    key_grad = jnp.concatenate([joined[0], joined[1]], axis=1)
    value_grad = jnp.concatenate([joined[2], joined[3]], axis=1)
    total = dot(key_grad, key_weight[...], 1, 1) + dot(value_grad, value_weight[...], 1, 1)
    for m in range(HELD):
        grad_latent[m] = total[m * LAT_DEV : (m + 1) * LAT_DEV]


def weight_kernel(parts, shares, out_grad, send):
    rows = jnp.concatenate([parts[e] for e in range(ENS)], axis=0)
    held = HELD * LAT_DEV
    for j in range(GROUPS):
        nodes = jnp.concatenate([shares[e, j * held : (j + 1) * held] for e in range(ENS)], axis=0)
        product = dot(nodes, rows, 0, 0).astype(LOW)
        for b in range(GROUP // SHARE):
            r = j * (GROUP // SHARE) + b
            z, xy = r // PLANE, r % PLANE
            at = slice(z * SHARE, (z + 1) * SHARE)
            send[xy, at, :COLS] = product[b * SHARE : (b + 1) * SHARE]
            send[xy, at, COLS:] = out_grad[r * SHARE : (r + 1) * SHARE]


def sum_kernel(parts, total):
    value = parts[0].astype(F32)
    for p in range(1, PLANE):
        value = value + parts[p].astype(F32)
    total[...] = value.astype(LOW)


def last_sum_kernel(parts, grad_latent, total):
    value = parts[0].astype(F32)
    for p in range(1, PLANE):
        value = value + parts[p].astype(F32)
    total[...] = value.astype(LOW)


def finish_kernel(parts, key_weight_grad, value_weight_grad, out_weight_grad):
    total = parts[0, :, COLS:].astype(F32)
    for e in range(1, ENS):
        total = total + parts[e, :, COLS:].astype(F32)
    out_weight_grad[...] = total[:, :VARS]
    for p in range(2):
        key_weight_grad[:, p * COLS : (p + 1) * COLS] = parts[p, :, :COLS].astype(F32)
        value_weight_grad[:, p * COLS : (p + 1) * COLS] = parts[2 + p, :, :COLS].astype(F32)


def whole(shape):
    return pl.BlockSpec(shape, lambda i: (0,) * len(shape))


def call(kernel, outs, scratch=(), specs=None, flops=10**8, bytes_accessed=4 * 10**6):
    def run(*operands):
        places = specs or {}
        return pl.pallas_call(
            kernel,
            grid=(1,),
            in_specs=[places.get(i, whole(value.shape)) for i, value in enumerate(operands)],
            out_specs=[whole(shape) for shape, _ in outs],
            out_shape=[jax.ShapeDtypeStruct(shape, kind) for shape, kind in outs],
            scratch_shapes=[pltpu.VMEM(shape, kind) for shape, kind in scratch],
            compiler_params=pltpu.CompilerParams(vmem_limit_bytes=40 * 2**20),
            cost_estimate=pl.CostEstimate(
                flops=flops, bytes_accessed=bytes_accessed, transcendentals=0
            ),
            name=kernel.__name__,
        )(*operands)

    return run


def band_shift(value, by):
    return lax.ppermute(value, BAND, [(i, i + by) for i in range(64) if 0 <= i + by < 64])


def on_device(grid_embed, latent, key_weight, value_weight, out_weight, target, edges):
    held = HELD * LAT_DEV
    out_rows = jnp.pad(out_weight, ((0, VARS_PAD - VARS), (0, 0)))
    upper_latent = band_shift(latent, -1)
    own_keys, own_values, count = call(
        own_kernel, [((held, D), LOW), ((held, D), LOW), ((GRID_DEV, GROUP), F32)]
    )(latent, key_weight, value_weight, edges)
    preds, share, normed_low, inverse, exps, damps, values = call(
        forward_kernel,
        [
            ((HELD, VARS_PAD, GRID_DEV), F32),
            ((PRED_ROW + VARS_PAD, GROUP), LOW),
            ((HELD, GRID_DEV, D), LOW),
            ((HELD, GRID_DEV, 128), F32),
            ((HELD, GRID_DEV, D), LOW),
            ((HELD, GRID_DEV, D), LOW),
            ((HELD * WINDOW, D), LOW),
        ],
        [((HELD * WINDOW, D), LOW), ((GRID_DEV, D), F32)],
    )(
        grid_embed, latent, upper_latent, key_weight, value_weight, out_rows,
        own_keys, own_values, count,
    )
    shares = lax.all_gather(share, "ens", axis=0)
    own, upper, out_grad = call(
        backward_kernel,
        [
            ((2, HELD, LAT_DEV, D), F32),
            ((2, HELD, LAT_DEV, D), LOW),
            ((D, VARS_PAD), LOW),
        ],
        [((GRID_DEV, D), F32), ((VARS_PAD, GRID_DEV), F32)],
        {4: pl.BlockSpec((ENS, VARS_PAD, GROUP), lambda i: (0, PRED_ROW // VARS_PAD, 0))},
    )(grid_embed, out_rows, target, preds, shares, normed_low, inverse, exps, damps, values)
    lower = band_shift(upper, 1)
    (joined,) = call(join_kernel, [((ENS, held, COLS), LOW)])(own, lower)
    (grad_latent,) = call(latent_kernel, [((HELD, LAT_DEV, D), F32)])(
        joined, key_weight, value_weight
    )
    parts = lax.all_to_all(joined, "ens", 0, 0, tiled=True)
    (send,) = call(
        weight_kernel,
        [((PLANE, 8 * SHARE, COLS + VARS_PAD), LOW)],
        specs={1: pl.BlockSpec((ENS, PRED_ROW, GROUP), lambda i: (0, 0, 0))},
    )(parts, shares, out_grad)
    parts = lax.all_to_all(send, ("x", "y"), 0, 0, tiled=True)
    (total,) = call(sum_kernel, [((8 * SHARE, COLS + VARS_PAD), LOW)])(parts)
    parts = lax.all_to_all(total.reshape(8, SHARE, COLS + VARS_PAD), "z", 0, 0, tiled=True)
    (total,) = call(
        last_sum_kernel,
        [((SHARE, COLS + VARS_PAD), LOW)],
        specs={1: pl.BlockSpec(memory_space=pl.ANY)},
    )(parts, grad_latent)
    parts = lax.all_gather(total, "ens", axis=0)
    results = call(finish_kernel, [((16, D), F32), ((16, D), F32), ((16, VARS), F32)])(parts)
    return (results[0], results[1], results[2], grad_latent)


def solution(mesh):
    wide = Mesh(mesh.devices.reshape(4, 8, 4, 2), ("ens", "z", "x", "y"))
    in_specs = (
        P("ens", BAND, None),
        P("ens", BAND, None),
        P(),
        P(),
        P(),
        P(None, BAND),
        P(None, BAND),
    )
    out_specs = (P(BAND, None), P(BAND, None), P(BAND, None), P("ens", BAND, None))
    return jax.shard_map(
        on_device, mesh=wide, in_specs=in_specs, out_specs=out_specs, check_vma=False
    )
```

```python
import jax
import jax.numpy as jnp
from jax import lax
from jax.experimental import pallas as pl
from jax.experimental.pallas import tpu as pltpu
from jax.sharding import Mesh
from jax.sharding import PartitionSpec as P

HEAD_DIM = 64
CAP = 5.0
DELTA_SQ = 0.0625
EPS = 1e-06

MEMBERS = 8
HELD = 2
GRID_DEV = 128
LAT_DEV = 32
WINDOW = 64
D = 1024
VARS = 100
VARS_PAD = 128
GROUP = 256
GROUPS = D // GROUP
BAND = ("z", "x", "y")
ENS = 4
NEAR = 8
FAR = 8
SHARE = 16
COLS = 2 * D // ENS
HELD_ROWS = HELD * LAT_DEV

F32 = jnp.float32
LOW = jnp.bfloat16


def slope(offset):
    return offset * lax.rsqrt(offset * offset + DELTA_SQ)


def dot(a, b, a_dim, b_dim):
    return lax.dot_general(a, b, (((a_dim,), (b_dim,)), ((), ())), preferred_element_type=F32)


def same_head():
    rows = lax.broadcasted_iota(jnp.int32, (GROUP, GROUP), 0) // HEAD_DIM
    cols = lax.broadcasted_iota(jnp.int32, (GROUP, GROUP), 1) // HEAD_DIM
    return rows == cols


def by_head(rows, same):
    return jnp.where(same, jnp.concatenate([rows] * 4, axis=0), jnp.zeros((), LOW))


def from_head(blocks):
    head = lax.broadcasted_iota(jnp.int32, (WINDOW, GROUP), 1) // HEAD_DIM
    total = blocks[:WINDOW]
    for h in range(1, 4):
        total = jnp.where(head == h, blocks[h * WINDOW : (h + 1) * WINDOW], total)
    return total


def own_kernel(latent, weights, edges, keys, values, count):
    rows = jnp.concatenate([latent[0], latent[1]], axis=0)
    keys[...] = dot(rows, weights[:D], 1, 0).astype(LOW)
    values[...] = dot(rows, weights[D:], 1, 0).astype(LOW)
    target = edges[0:1, :]
    local = jnp.where(target >= 0, target & (GRID_DEV - 1), -1)
    source = edges[1:2, :] - (target >> 7) * LAT_DEV
    slots = edges.shape[1]
    into = (lax.broadcasted_iota(jnp.int32, (GRID_DEV, slots), 0) == local).astype(F32).astype(LOW)
    node = lax.broadcasted_iota(jnp.int32, (GROUP, slots), 0) & (WINDOW - 1)
    out_of = (node == source).astype(F32).astype(LOW)
    count[...] = dot(into, out_of, 1, 1)


def forward_kernel(
    embed, lat_up, weights, out_weight, own_keys, own_values, edge_count,
    preds, share, normed_low, inverse, exps, damps, values,
    keys, mixed,
):
    rows = jnp.concatenate([lat_up[0], lat_up[1]], axis=0)
    for own_rows, weight, window in ((own_keys, 0, keys), (own_values, D, values)):
        upper_rows = dot(rows, weights[weight : weight + D], 1, 0).astype(LOW)
        for m in range(HELD):
            window[m * WINDOW : m * WINDOW + LAT_DEV] = own_rows[m * LAT_DEV : (m + 1) * LAT_DEV]
            window[m * WINDOW + LAT_DEV : (m + 1) * WINDOW] = upper_rows[m * LAT_DEV : (m + 1) * LAT_DEV]
    count = edge_count[...]
    same = same_head()
    ones = same.astype(F32).astype(LOW)
    for m in range(HELD):
        square = jnp.zeros((GRID_DEV, 1), F32)
        for j in range(GROUPS):
            cols = slice(j * GROUP, (j + 1) * GROUP)
            query = embed[m, :, cols]
            key = by_head(keys[m * WINDOW : (m + 1) * WINDOW, cols], same)
            value = by_head(values[m * WINDOW : (m + 1) * WINDOW, cols], same)
            bent = jnp.tanh(dot(query, key, 1, 1) * (HEAD_DIM**-0.5 / CAP))
            exp = (count * jnp.exp(CAP * bent)).astype(LOW)
            exps[m, :, cols] = exp
            damps[m, :, cols] = ((1.0 - bent * bent) * HEAD_DIM**-0.5).astype(LOW)
            attended = dot(exp, value, 1, 0) / dot(exp, ones, 1, 0)
            sums = query.astype(F32) + attended
            mixed[:, cols] = sums
            square = square + jnp.sum(sums * sums, axis=1, keepdims=True)
        inv = lax.rsqrt(square * (1.0 / D) + EPS)
        low = (mixed[...] * inv).astype(LOW)
        normed_low[m] = low
        inverse[m] = jnp.broadcast_to(inv, (GRID_DEV, 128))
        pred = dot(out_weight[...], low, 1, 1)
        preds[m] = pred
        share[m] = pred.astype(LOW)


def backward_kernel(
    embed, out_weight, target, preds, every, normed_low, inverse, exps, damps, values,
    own, upper, out_grad,
    grad, truth,
):
    truth[...] = jnp.zeros((VARS_PAD, GRID_DEV), F32)
    truth[:VARS, :] = target[...]
    same = same_head()
    ones = same.astype(F32).astype(LOW)
    pred_grads = []
    for m in range(HELD):
        pred = preds[m]
        pair = jnp.zeros((VARS_PAD, GRID_DEV), F32)
        for e in range(MEMBERS // HELD):
            for k in range(HELD):
                pair = pair + slope(pred - every[e, k].astype(F32))
        for k in range(HELD):
            pair = pair - slope(pred - preds[k].astype(LOW).astype(F32))
            if k != m:
                pair = pair + slope(pred - preds[k])
        base = slope(pred - truth[...]) * (1.0 / MEMBERS)
        pred_grads.append((base - pair * (1.0 / (MEMBERS * (MEMBERS - 1)))).astype(LOW))
    both = jnp.concatenate(pred_grads, axis=1)
    lows = jnp.concatenate([normed_low[0], normed_low[1]], axis=0)
    out_grad[...] = jnp.transpose(dot(both, lows, 1, 0)).astype(LOW)
    for m in range(HELD):
        slant = jnp.zeros((GRID_DEV, 1), F32)
        for j in range(GROUPS):
            cols = slice(j * GROUP, (j + 1) * GROUP)
            part = dot(pred_grads[m], out_weight[:, cols], 0, 0)
            grad[:, cols] = part
            slant = slant + jnp.sum(part * normed_low[m, :, cols].astype(F32), axis=1, keepdims=True)
        slant = slant * (1.0 / D)
        inv = inverse[m][:, :1]
        for j in range(GROUPS):
            cols = slice(j * GROUP, (j + 1) * GROUP)
            mixed_grad = (inv * (grad[:, cols] - normed_low[m, :, cols].astype(F32) * slant)).astype(LOW)
            value = by_head(values[m * WINDOW : (m + 1) * WINDOW, cols], same)
            exp = exps[m, :, cols]
            weight = exp.astype(F32) / dot(exp, ones, 1, 0)
            weight_grad = dot(mixed_grad, value, 1, 1)
            term = weight * weight_grad
            high = term.astype(LOW)
            rest = (term - high.astype(F32)).astype(LOW)
            inner = dot(high, ones, 1, 0) + dot(rest, ones, 1, 0)
            raw_grad = (weight * (weight_grad - inner) * damps[m, :, cols].astype(F32)).astype(LOW)
            key_part = from_head(dot(raw_grad, embed[m, :, cols], 0, 0))
            value_part = from_head(dot(weight.astype(LOW), mixed_grad, 0, 0))
            own[0, m, :, cols] = key_part[:LAT_DEV]
            own[1, m, :, cols] = value_part[:LAT_DEV]
            upper[0, m, :, cols] = key_part[LAT_DEV:].astype(LOW)
            upper[1, m, :, cols] = value_part[LAT_DEV:].astype(LOW)


def join_kernel(me, own, lower, joined, next1, next2, next3):
    for which in range(2):
        for m in range(HELD):
            total = (own[which, m] + lower[which, m].astype(F32)).astype(LOW)
            for p in range(2):
                joined[2 * which + p, m * LAT_DEV : (m + 1) * LAT_DEV, :] = total[
                    :, p * COLS : (p + 1) * COLS
                ]
    for k, block in ((1, next1), (2, next2), (3, next3)):
        block[...] = joined[(me[0] + k) & (ENS - 1)]


def latent_kernel(joined, key_weight, value_weight, grad_latent, token):
    key_grad = jnp.concatenate([joined[0], joined[1]], axis=1)
    value_grad = jnp.concatenate([joined[2], joined[3]], axis=1)
    total = dot(key_grad, key_weight[...], 1, 1) + dot(value_grad, value_weight[...], 1, 1)
    for m in range(HELD):
        grad_latent[m] = total[m * LAT_DEV : (m + 1) * LAT_DEV]
    token[...] = total[:8, :128]


def weight_kernel(
    me, joined, last1, last2, last3, nodes, nodes1, nodes2, nodes3, out_grad, token, send
):
    rows = jnp.concatenate([joined[me[0]], last1[...], last2[...], last3[...]], axis=0)
    for j in range(GROUPS):
        cols = slice(j * GROUP, (j + 1) * GROUP)
        held = [nodes[0, :, cols], nodes[1, :, cols]]
        left = jnp.concatenate(
            held + [block[m, :, cols] for block in (nodes1, nodes2, nodes3) for m in range(HELD)],
            axis=0,
        )
        product = dot(left, rows, 0, 0).astype(LOW)
        for b in range(GROUP // SHARE):
            r = j * (GROUP // SHARE) + b
            far, near = r // NEAR, r % NEAR
            at = slice(far * SHARE, (far + 1) * SHARE)
            send[near, at, :COLS] = product[b * SHARE : (b + 1) * SHARE]
            send[near, at, COLS:] = out_grad[r * SHARE : (r + 1) * SHARE]


def sum_kernel(parts, total):
    value = parts[0].astype(F32)
    for p in range(1, parts.shape[0]):
        value = value + parts[p].astype(F32)
    total[...] = value.astype(LOW)


def finish_kernel(parts, key_weight_grad, value_weight_grad, out_weight_grad):
    total = parts[0, :, COLS:].astype(F32)
    for e in range(1, ENS):
        total = total + parts[e, :, COLS:].astype(F32)
    out_weight_grad[...] = total[:, :VARS]
    for p in range(2):
        key_weight_grad[:, p * COLS : (p + 1) * COLS] = parts[p, :, :COLS].astype(F32)
        value_weight_grad[:, p * COLS : (p + 1) * COLS] = parts[2 + p, :, :COLS].astype(F32)


def whole(shape):
    return pl.BlockSpec(shape, lambda i: (0,) * len(shape))


def call(kernel, outs, scratch=(), specs=None, flops=10**8, bytes_accessed=4 * 10**6):
    def run(*operands):
        places = specs or {}
        return pl.pallas_call(
            kernel,
            grid=(1,),
            in_specs=[places.get(i, whole(value.shape)) for i, value in enumerate(operands)],
            out_specs=[whole(shape) for shape, _ in outs],
            out_shape=[jax.ShapeDtypeStruct(shape, kind) for shape, kind in outs],
            scratch_shapes=[pltpu.VMEM(shape, kind) for shape, kind in scratch],
            compiler_params=pltpu.CompilerParams(vmem_limit_bytes=40 * 2**20),
            cost_estimate=pl.CostEstimate(
                flops=flops, bytes_accessed=bytes_accessed, transcendentals=0
            ),
            name=kernel.__name__,
        )(*operands)

    return run


def band_shift(value, by):
    return lax.ppermute(value, BAND, [(i, i + by) for i in range(64) if 0 <= i + by < 64])


def ens_shift(value, by):
    return lax.ppermute(value, "ens", [(e, (e + by) % ENS) for e in range(ENS)])


def on_device(grid_embed, latent, key_weight, value_weight, out_weight, target, edges):
    out_rows = jnp.pad(out_weight, ((0, VARS_PAD - VARS), (0, 0)))
    upper_latent = band_shift(latent, -1)
    nodes1, nodes2, nodes3 = (ens_shift(latent, k) for k in (1, 2, 3))
    weights = jnp.concatenate([key_weight, value_weight], axis=0)
    own_keys, own_values, count = call(
        own_kernel, [((HELD_ROWS, D), LOW), ((HELD_ROWS, D), LOW), ((GRID_DEV, GROUP), F32)]
    )(latent, weights, edges)
    preds, share, normed_low, inverse, exps, damps, values = call(
        forward_kernel,
        [
            ((HELD, VARS_PAD, GRID_DEV), F32),
            ((HELD, VARS_PAD, GRID_DEV), LOW),
            ((HELD, GRID_DEV, D), LOW),
            ((HELD, GRID_DEV, 128), F32),
            ((HELD, GRID_DEV, D), LOW),
            ((HELD, GRID_DEV, D), LOW),
            ((HELD * WINDOW, D), LOW),
        ],
        [((HELD * WINDOW, D), LOW), ((GRID_DEV, D), F32)],
    )(
        grid_embed, upper_latent, weights, out_rows,
        own_keys, own_values, count,
    )
    me = lax.axis_index("ens").reshape(1)
    shares = lax.all_gather(share, "ens", axis=0)
    own, upper, out_grad = call(
        backward_kernel,
        [
            ((2, HELD, LAT_DEV, D), F32),
            ((2, HELD, LAT_DEV, D), LOW),
            ((D, VARS_PAD), LOW),
        ],
        [((GRID_DEV, D), F32), ((VARS_PAD, GRID_DEV), F32)],
    )(grid_embed, out_rows, target, preds, shares, normed_low, inverse, exps, damps, values)
    lower = band_shift(upper, 1)
    scalar = {0: pl.BlockSpec(memory_space=pltpu.SMEM)}
    block = (HELD_ROWS, COLS)
    joined, next1, next2, next3 = call(
        join_kernel,
        [((ENS, *block), LOW)] + [(block, LOW)] * 3,
        specs=scalar,
    )(me, own, lower)
    last1, last2, last3 = (ens_shift(v, k) for k, v in ((1, next1), (2, next2), (3, next3)))
    grad_latent, token = call(latent_kernel, [((HELD, LAT_DEV, D), F32), ((8, 128), F32)])(
        joined, key_weight, value_weight
    )
    (send,) = call(weight_kernel, [((NEAR, FAR * SHARE, COLS + VARS_PAD), LOW)], specs=scalar)(
        me, joined, last1, last2, last3, latent, nodes1, nodes2, nodes3, out_grad, token
    )
    parts = lax.all_to_all(send, ("x", "y"), 0, 0, tiled=True)
    (total,) = call(sum_kernel, [((FAR * SHARE, COLS + VARS_PAD), LOW)])(parts)
    parts = lax.all_to_all(total.reshape(FAR, SHARE, COLS + VARS_PAD), "z", 0, 0, tiled=True)
    (total,) = call(sum_kernel, [((SHARE, COLS + VARS_PAD), LOW)])(parts)
    parts = lax.all_gather(total, "ens", axis=0)
    results = call(finish_kernel, [((16, D), F32), ((16, D), F32), ((16, VARS), F32)])(parts)
    return (results[0], results[1], results[2], grad_latent)


def solution(mesh):
    wide = Mesh(mesh.devices.reshape(4, 8, 4, 2), ("ens", *BAND))
    in_specs = (
        P("ens", BAND, None),
        P("ens", BAND, None),
        P(),
        P(),
        P(),
        P(None, BAND),
        P(None, BAND),
    )
    out_specs = (P(BAND, None), P(BAND, None), P(BAND, None), P("ens", BAND, None))
    return jax.shard_map(
        on_device, mesh=wide, in_specs=in_specs, out_specs=out_specs, check_vma=False
    )
```

```python
import jax
import jax.numpy as jnp
from jax import lax
from jax.experimental import pallas as pl
from jax.experimental.pallas import tpu as pltpu
from jax.sharding import Mesh
from jax.sharding import PartitionSpec as P

HEAD_DIM = 64
CAP = 5.0
DELTA_SQ = 0.0625
EPS = 1e-06

MEMBERS = 8
HELD = 2
GRID_DEV = 128
LAT_DEV = 32
WINDOW = 64
D = 1024
VARS = 100
VARS_PAD = 128
GROUP = 256
GROUPS = D // GROUP
BAND = ("z", "x", "y")
ENS = 4
NEAR = 8
FAR = 8
SHARE = 16
COLS = 2 * D // ENS
HELD_ROWS = HELD * LAT_DEV
PRED_ROW = HELD_ROWS * GROUPS

F32 = jnp.float32
LOW = jnp.bfloat16


def slope(offset):
    return offset * lax.rsqrt(offset * offset + DELTA_SQ)


def dot(a, b, a_dim, b_dim):
    return lax.dot_general(a, b, (((a_dim,), (b_dim,)), ((), ())), preferred_element_type=F32)


def same_head():
    rows = lax.broadcasted_iota(jnp.int32, (GROUP, GROUP), 0) // HEAD_DIM
    cols = lax.broadcasted_iota(jnp.int32, (GROUP, GROUP), 1) // HEAD_DIM
    return rows == cols


def by_head(rows, same):
    return jnp.where(same, jnp.concatenate([rows] * 4, axis=0), jnp.zeros((), LOW))


def from_head(blocks):
    head = lax.broadcasted_iota(jnp.int32, (WINDOW, GROUP), 1) // HEAD_DIM
    total = blocks[:WINDOW]
    for h in range(1, 4):
        total = jnp.where(head == h, blocks[h * WINDOW : (h + 1) * WINDOW], total)
    return total


def own_kernel(latent, weights, edges, keys, values, count):
    rows = jnp.concatenate([latent[0], latent[1]], axis=0)
    keys[...] = dot(rows, weights[:D], 1, 0).astype(LOW)
    values[...] = dot(rows, weights[D:], 1, 0).astype(LOW)
    target = edges[0:1, :]
    local = jnp.where(target >= 0, target & (GRID_DEV - 1), -1)
    source = edges[1:2, :] - (target >> 7) * LAT_DEV
    slots = edges.shape[1]
    into = (lax.broadcasted_iota(jnp.int32, (GRID_DEV, slots), 0) == local).astype(F32).astype(LOW)
    node = lax.broadcasted_iota(jnp.int32, (GROUP, slots), 0) & (WINDOW - 1)
    out_of = (node == source).astype(F32).astype(LOW)
    count[...] = dot(into, out_of, 1, 1)


def forward_kernel(
    embed, lat_up, weights, out_weight, own_keys, own_values, edge_count,
    preds, share, normed_low, inverse, exps, damps, values,
    keys, mixed,
):
    rows = jnp.concatenate([lat_up[0], lat_up[1]], axis=0)
    for own_rows, weight, window in ((own_keys, 0, keys), (own_values, D, values)):
        upper_rows = dot(rows, weights[weight : weight + D], 1, 0).astype(LOW)
        for m in range(HELD):
            window[m * WINDOW : m * WINDOW + LAT_DEV] = own_rows[m * LAT_DEV : (m + 1) * LAT_DEV]
            window[m * WINDOW + LAT_DEV : (m + 1) * WINDOW] = upper_rows[m * LAT_DEV : (m + 1) * LAT_DEV]
    count = edge_count[...]
    same = same_head()
    ones = same.astype(F32).astype(LOW)
    for m in range(HELD):
        square = jnp.zeros((GRID_DEV, 1), F32)
        for j in range(GROUPS):
            cols = slice(j * GROUP, (j + 1) * GROUP)
            start = j * HELD_ROWS + m * LAT_DEV
            share[start : start + LAT_DEV] = lat_up[m, :, cols]
            query = embed[m, :, cols]
            key = by_head(keys[m * WINDOW : (m + 1) * WINDOW, cols], same)
            value = by_head(values[m * WINDOW : (m + 1) * WINDOW, cols], same)
            bent = jnp.tanh(dot(query, key, 1, 1) * (HEAD_DIM**-0.5 / CAP))
            exp = (count * jnp.exp(CAP * bent)).astype(LOW)
            exps[m, :, cols] = exp
            damps[m, :, cols] = ((1.0 - bent * bent) * HEAD_DIM**-0.5).astype(LOW)
            attended = dot(exp, value, 1, 0) / dot(exp, ones, 1, 0)
            sums = query.astype(F32) + attended
            mixed[:, cols] = sums
            square = square + jnp.sum(sums * sums, axis=1, keepdims=True)
        inv = lax.rsqrt(square * (1.0 / D) + EPS)
        low = (mixed[...] * inv).astype(LOW)
        normed_low[m] = low
        inverse[m] = jnp.broadcast_to(inv, (GRID_DEV, 128))
        pred = dot(out_weight[...], low, 1, 1)
        preds[m] = pred
        share[PRED_ROW:, m * GRID_DEV : (m + 1) * GRID_DEV] = pred.astype(LOW)


def backward_kernel(
    me, embed, out_weight, target, preds, every, normed_low, inverse, exps, damps, values,
    halves, next1, next2, next3, out_grad,
    grad, truth,
):
    truth[...] = jnp.zeros((VARS_PAD, GRID_DEV), F32)
    truth[:VARS, :] = target[...]
    same = same_head()
    ones = same.astype(F32).astype(LOW)
    pred_grads = []
    for m in range(HELD):
        pred = preds[m]
        pair = jnp.zeros((VARS_PAD, GRID_DEV), F32)
        for e in range(MEMBERS // HELD):
            for k in range(HELD):
                pair = pair + slope(pred - every[e, :, k * GRID_DEV : (k + 1) * GRID_DEV].astype(F32))
        for k in range(HELD):
            pair = pair - slope(pred - preds[k].astype(LOW).astype(F32))
            if k != m:
                pair = pair + slope(pred - preds[k])
        base = slope(pred - truth[...]) * (1.0 / MEMBERS)
        pred_grads.append((base - pair * (1.0 / (MEMBERS * (MEMBERS - 1)))).astype(LOW))
    both = jnp.concatenate(pred_grads, axis=1)
    lows = jnp.concatenate([normed_low[0], normed_low[1]], axis=0)
    out_grad[...] = jnp.transpose(dot(both, lows, 1, 0)).astype(LOW)
    for m in range(HELD):
        slant = jnp.zeros((GRID_DEV, 1), F32)
        for j in range(GROUPS):
            cols = slice(j * GROUP, (j + 1) * GROUP)
            part = dot(pred_grads[m], out_weight[:, cols], 0, 0)
            grad[:, cols] = part
            slant = slant + jnp.sum(part * normed_low[m, :, cols].astype(F32), axis=1, keepdims=True)
        slant = slant * (1.0 / D)
        inv = inverse[m][:, :1]
        for j in range(GROUPS):
            cols = slice(j * GROUP, (j + 1) * GROUP)
            mixed_grad = (inv * (grad[:, cols] - normed_low[m, :, cols].astype(F32) * slant)).astype(LOW)
            value = by_head(values[m * WINDOW : (m + 1) * WINDOW, cols], same)
            exp = exps[m, :, cols]
            weight = exp.astype(F32) / dot(exp, ones, 1, 0)
            weight_grad = dot(mixed_grad, value, 1, 1)
            term = weight * weight_grad
            high = term.astype(LOW)
            rest = (term - high.astype(F32)).astype(LOW)
            inner = dot(high, ones, 1, 0) + dot(rest, ones, 1, 0)
            raw_grad = (weight * (weight_grad - inner) * damps[m, :, cols].astype(F32)).astype(LOW)
            key_part = from_head(dot(raw_grad, embed[m, :, cols], 0, 0))
            value_part = from_head(dot(weight.astype(LOW), mixed_grad, 0, 0))
            at = slice(j % 2 * GROUP, (j % 2 + 1) * GROUP)
            for p, part in ((j // 2, key_part), (2 + j // 2, value_part)):
                start = m * LAT_DEV
                halves[p, start : start + LAT_DEV, at] = part[:LAT_DEV].astype(LOW)
                start = start + HELD_ROWS
                halves[p, start : start + LAT_DEV, at] = part[LAT_DEV:].astype(LOW)
    for k, block in ((1, next1), (2, next2), (3, next3)):
        block[...] = halves[me[0] ^ k]


def latent_kernel(halves, key_weight, value_weight, own, upper):
    key_grad = jnp.concatenate([halves[0], halves[1]], axis=1)
    value_grad = jnp.concatenate([halves[2], halves[3]], axis=1)
    total = dot(key_grad, key_weight[...], 1, 1) + dot(value_grad, value_weight[...], 1, 1)
    own[...] = total[:HELD_ROWS]
    upper[...] = total[HELD_ROWS:].astype(LOW)


def weight_kernel(
    me, halves, last1, last2, last3, nodes, nodes1, nodes2, nodes3, shares, out_grad, upper, send
):
    rows = jnp.concatenate([halves[me[0]], last1[...], last2[...], last3[...]], axis=0)
    for j in range(GROUPS):
        cols = slice(j * GROUP, (j + 1) * GROUP)
        at = slice(j * HELD_ROWS, (j + 1) * HELD_ROWS)
        left = []
        for k, block in enumerate((nodes, nodes1, nodes2, nodes3)):
            left += [block[0, :, cols], block[1, :, cols], shares[me[0] ^ k, at]]
        left = jnp.concatenate(left, axis=0)
        product = dot(left, rows, 0, 0).astype(LOW)
        for b in range(GROUP // SHARE):
            r = j * (GROUP // SHARE) + b
            far, near = r // NEAR, r % NEAR
            at = slice(far * SHARE, (far + 1) * SHARE)
            send[near, at, :COLS] = product[b * SHARE : (b + 1) * SHARE]
            send[near, at, COLS:] = out_grad[r * SHARE : (r + 1) * SHARE]


def sum_kernel(parts, total):
    value = parts[0].astype(F32)
    for p in range(1, parts.shape[0]):
        value = value + parts[p].astype(F32)
    total[...] = value.astype(LOW)


def finish_kernel(
    parts, own, lower, key_weight_grad, value_weight_grad, out_weight_grad, grad_latent
):
    for m in range(HELD):
        rows = slice(m * LAT_DEV, (m + 1) * LAT_DEV)
        grad_latent[m] = own[rows] + lower[rows].astype(F32)
    total = parts[0, :, COLS:].astype(F32)
    for e in range(1, ENS):
        total = total + parts[e, :, COLS:].astype(F32)
    out_weight_grad[...] = total[:, :VARS]
    for p in range(2):
        key_weight_grad[:, p * COLS : (p + 1) * COLS] = parts[p, :, :COLS].astype(F32)
        value_weight_grad[:, p * COLS : (p + 1) * COLS] = parts[2 + p, :, :COLS].astype(F32)


def whole(shape):
    return pl.BlockSpec(shape, lambda i: (0,) * len(shape))


def call(kernel, outs, scratch=(), specs=None, flops=10**8, bytes_accessed=4 * 10**6):
    def run(*operands):
        places = specs or {}
        return pl.pallas_call(
            kernel,
            grid=(1,),
            in_specs=[places.get(i, whole(value.shape)) for i, value in enumerate(operands)],
            out_specs=[whole(shape) for shape, _ in outs],
            out_shape=[jax.ShapeDtypeStruct(shape, kind) for shape, kind in outs],
            scratch_shapes=[pltpu.VMEM(shape, kind) for shape, kind in scratch],
            compiler_params=pltpu.CompilerParams(vmem_limit_bytes=40 * 2**20),
            cost_estimate=pl.CostEstimate(
                flops=flops, bytes_accessed=bytes_accessed, transcendentals=0
            ),
            name=kernel.__name__,
        )(*operands)

    return run


def band_shift(value, by):
    return lax.ppermute(value, BAND, [(i, i + by) for i in range(64) if 0 <= i + by < 64])


def ens_swap(value, k):
    return lax.ppermute(value, "ens", [(e, e ^ k) for e in range(ENS)])


def on_device(grid_embed, latent, key_weight, value_weight, out_weight, target, edges):
    out_rows = jnp.pad(out_weight, ((0, VARS_PAD - VARS), (0, 0)))
    upper_latent = band_shift(latent, -1)
    nodes1, nodes2 = ens_swap(latent, 1), ens_swap(latent, 2)
    nodes3 = ens_swap(nodes2, 1)
    weights = jnp.concatenate([key_weight, value_weight], axis=0)
    own_keys, own_values, count = call(
        own_kernel, [((HELD_ROWS, D), LOW), ((HELD_ROWS, D), LOW), ((GRID_DEV, GROUP), F32)]
    )(latent, weights, edges)
    preds, share, normed_low, inverse, exps, damps, values = call(
        forward_kernel,
        [
            ((HELD, VARS_PAD, GRID_DEV), F32),
            ((PRED_ROW + VARS_PAD, GROUP), LOW),
            ((HELD, GRID_DEV, D), LOW),
            ((HELD, GRID_DEV, 128), F32),
            ((HELD, GRID_DEV, D), LOW),
            ((HELD, GRID_DEV, D), LOW),
            ((HELD * WINDOW, D), LOW),
        ],
        [((HELD * WINDOW, D), LOW), ((GRID_DEV, D), F32)],
    )(
        grid_embed, upper_latent, weights, out_rows,
        own_keys, own_values, count,
    )
    me = lax.axis_index("ens").reshape(1)
    shares = lax.all_gather(share, "ens", axis=0)
    block = (2 * HELD_ROWS, COLS)
    scalar = {0: pl.BlockSpec(memory_space=pltpu.SMEM)}
    halves, next1, next2, next3, out_grad = call(
        backward_kernel,
        [((ENS, *block), LOW)] + [(block, LOW)] * 3 + [((D, VARS_PAD), LOW)],
        [((GRID_DEV, D), F32), ((VARS_PAD, GRID_DEV), F32)],
        {**scalar, 5: pl.BlockSpec((ENS, VARS_PAD, GROUP), lambda i: (0, PRED_ROW // VARS_PAD, 0))},
    )(me, grid_embed, out_rows, target, preds, shares, normed_low, inverse, exps, damps, values)
    last1, last2, last3 = (ens_swap(v, k) for k, v in ((1, next1), (2, next2), (3, next3)))
    own, upper = call(latent_kernel, [((HELD_ROWS, D), F32), ((HELD_ROWS, D), LOW)])(
        halves, key_weight, value_weight
    )
    lower = band_shift(upper, 1)
    (send,) = call(
        weight_kernel,
        [((NEAR, FAR * SHARE, COLS + VARS_PAD), LOW)],
        specs={
            **scalar,
            9: pl.BlockSpec((ENS, PRED_ROW, GROUP), lambda i: (0, 0, 0)),
            11: pl.BlockSpec((16, 128), lambda i: (0, 0)),
        },
    )(
        me, halves, last1, last2, last3, latent, nodes1, nodes2, nodes3, shares, out_grad, upper
    )
    parts = lax.all_to_all(send, ("x", "y"), 0, 0, tiled=True)
    (total,) = call(sum_kernel, [((FAR * SHARE, COLS + VARS_PAD), LOW)])(parts)
    parts = lax.all_to_all(total.reshape(FAR, SHARE, COLS + VARS_PAD), "z", 0, 0, tiled=True)
    (total,) = call(sum_kernel, [((SHARE, COLS + VARS_PAD), LOW)])(parts)
    parts = lax.all_gather(total, "ens", axis=0)
    return tuple(
        call(
            finish_kernel,
            [((16, D), F32), ((16, D), F32), ((16, VARS), F32), ((HELD, LAT_DEV, D), F32)],
        )(parts, own, lower)
    )


def solution(mesh):
    wide = Mesh(mesh.devices.reshape(4, 8, 4, 2), ("ens", *BAND))
    in_specs = (
        P("ens", BAND, None),
        P("ens", BAND, None),
        P(),
        P(),
        P(),
        P(None, BAND),
        P(None, BAND),
    )
    out_specs = (P(BAND, None), P(BAND, None), P(BAND, None), P("ens", BAND, None))
    return jax.shard_map(
        on_device, mesh=wide, in_specs=in_specs, out_specs=out_specs, check_vma=False
    )
```

```python
import jax
import jax.numpy as jnp
from jax import lax
from jax.experimental import pallas as pl
from jax.experimental.pallas import tpu as pltpu
from jax.sharding import Mesh
from jax.sharding import PartitionSpec as P

HEAD_DIM = 64
CAP = 5.0
DELTA_SQ = 0.0625
EPS = 1e-06

MEMBERS = 8
HELD = 2
GRID_DEV = 128
LAT_DEV = 32
WINDOW = 64
D = 1024
VARS = 100
VARS_PAD = 128
GROUP = 256
GROUPS = D // GROUP
BAND = ("z", "x", "y")
ENS = 4
NEAR = 8
FAR = 8
SHARE = 16
COLS = 2 * D // ENS
HELD_ROWS = HELD * LAT_DEV
PRED_ROW = HELD_ROWS * GROUPS

F32 = jnp.float32
LOW = jnp.bfloat16


def slope(offset):
    return offset * lax.rsqrt(offset * offset + DELTA_SQ)


def dot(a, b, a_dim, b_dim):
    return lax.dot_general(a, b, (((a_dim,), (b_dim,)), ((), ())), preferred_element_type=F32)


def same_head():
    rows = lax.broadcasted_iota(jnp.int32, (GROUP, GROUP), 0) // HEAD_DIM
    cols = lax.broadcasted_iota(jnp.int32, (GROUP, GROUP), 1) // HEAD_DIM
    return rows == cols


def by_head(rows, same):
    return jnp.where(same, jnp.concatenate([rows] * 4, axis=0), jnp.zeros((), LOW))


def from_head(blocks):
    head = lax.broadcasted_iota(jnp.int32, (WINDOW, GROUP), 1) // HEAD_DIM
    total = blocks[:WINDOW]
    for h in range(1, 4):
        total = jnp.where(head == h, blocks[h * WINDOW : (h + 1) * WINDOW], total)
    return total


def own_kernel(latent, edges, key_left, key_right, keys, count):
    rows = jnp.concatenate([latent[0], latent[1]], axis=0)
    keys[:, : D // 2] = dot(rows, key_left[...], 1, 0).astype(LOW)
    keys[:, D // 2 :] = dot(rows, key_right[...], 1, 0).astype(LOW)
    target = edges[0:1, :]
    local = jnp.where(target >= 0, target & (GRID_DEV - 1), -1)
    source = edges[1:2, :] - (target >> 7) * LAT_DEV
    slots = edges.shape[1]
    into = (lax.broadcasted_iota(jnp.int32, (GRID_DEV, slots), 0) == local).astype(F32).astype(LOW)
    node = lax.broadcasted_iota(jnp.int32, (GROUP, slots), 0) & (WINDOW - 1)
    out_of = (node == source).astype(F32).astype(LOW)
    count[...] = dot(into, out_of, 1, 1)


def forward_kernel(
    embed, latent, lat_up, key_left, key_right, value_weight, out_weight, own_keys, edge_count,
    preds, share, normed_low, inverse, exps, damps, values,
    keys, mixed,
):
    rows = jnp.concatenate([latent[0], lat_up[0], latent[1], lat_up[1]], axis=0)
    values[...] = dot(rows, value_weight[...], 1, 0).astype(LOW)
    rows = jnp.concatenate([lat_up[0], lat_up[1]], axis=0)
    for c, weight in enumerate((key_left, key_right)):
        cols = slice(c * (D // 2), (c + 1) * (D // 2))
        upper_rows = dot(rows, weight[...], 1, 0).astype(LOW)
        for m in range(HELD):
            part = slice(m * LAT_DEV, (m + 1) * LAT_DEV)
            keys[m * WINDOW : m * WINDOW + LAT_DEV, cols] = own_keys[part, cols]
            keys[m * WINDOW + LAT_DEV : (m + 1) * WINDOW, cols] = upper_rows[part]
    count = edge_count[...]
    same = same_head()
    ones = same.astype(F32).astype(LOW)
    for m in range(HELD):
        square = jnp.zeros((GRID_DEV, 1), F32)
        for j in range(GROUPS):
            cols = slice(j * GROUP, (j + 1) * GROUP)
            start = j * HELD_ROWS + m * LAT_DEV
            share[start : start + LAT_DEV] = lat_up[m, :, cols]
            query = embed[m, :, cols]
            key = by_head(keys[m * WINDOW : (m + 1) * WINDOW, cols], same)
            value = by_head(values[m * WINDOW : (m + 1) * WINDOW, cols], same)
            bent = jnp.tanh(dot(query, key, 1, 1) * (HEAD_DIM**-0.5 / CAP))
            exp = (count * jnp.exp(CAP * bent)).astype(LOW)
            exps[m, :, cols] = exp
            damps[m, :, cols] = ((1.0 - bent * bent) * HEAD_DIM**-0.5).astype(LOW)
            attended = dot(exp, value, 1, 0) / dot(exp, ones, 1, 0)
            sums = query.astype(F32) + attended
            mixed[:, cols] = sums
            square = square + jnp.sum(sums * sums, axis=1, keepdims=True)
        inv = lax.rsqrt(square * (1.0 / D) + EPS)
        low = (mixed[...] * inv).astype(LOW)
        normed_low[m] = low
        inverse[m] = jnp.broadcast_to(inv, (GRID_DEV, 128))
        pred = dot(out_weight[...], low, 1, 1)
        preds[m] = pred
        share[PRED_ROW:, m * GRID_DEV : (m + 1) * GRID_DEV] = pred.astype(LOW)


def backward_kernel(
    me, embed, out_weight, target, preds, every, normed_low, inverse, exps, damps, values,
    halves, next1, next2, next3, out_grad,
    grad, truth,
):
    truth[...] = jnp.zeros((VARS_PAD, GRID_DEV), F32)
    truth[:VARS, :] = target[...]
    same = same_head()
    ones = same.astype(F32).astype(LOW)
    pred_grads = []
    for m in range(HELD):
        pred = preds[m]
        pair = jnp.zeros((VARS_PAD, GRID_DEV), F32)
        for e in range(MEMBERS // HELD):
            for k in range(HELD):
                pair = pair + slope(pred - every[e, :, k * GRID_DEV : (k + 1) * GRID_DEV].astype(F32))
        for k in range(HELD):
            pair = pair - slope(pred - preds[k].astype(LOW).astype(F32))
            if k != m:
                pair = pair + slope(pred - preds[k])
        base = slope(pred - truth[...]) * (1.0 / MEMBERS)
        pred_grads.append((base - pair * (1.0 / (MEMBERS * (MEMBERS - 1)))).astype(LOW))
    both = jnp.concatenate(pred_grads, axis=1)
    lows = jnp.concatenate([normed_low[0], normed_low[1]], axis=0)
    out_grad[...] = jnp.transpose(dot(both, lows, 1, 0)).astype(LOW)
    for m in range(HELD):
        slant = jnp.zeros((GRID_DEV, 1), F32)
        for j in range(GROUPS):
            cols = slice(j * GROUP, (j + 1) * GROUP)
            part = dot(pred_grads[m], out_weight[:, cols], 0, 0)
            grad[:, cols] = part
            slant = slant + jnp.sum(part * normed_low[m, :, cols].astype(F32), axis=1, keepdims=True)
        slant = slant * (1.0 / D)
        inv = inverse[m][:, :1]
        for j in range(GROUPS):
            cols = slice(j * GROUP, (j + 1) * GROUP)
            mixed_grad = (inv * (grad[:, cols] - normed_low[m, :, cols].astype(F32) * slant)).astype(LOW)
            value = by_head(values[m * WINDOW : (m + 1) * WINDOW, cols], same)
            exp = exps[m, :, cols]
            weight = exp.astype(F32) / dot(exp, ones, 1, 0)
            weight_grad = dot(mixed_grad, value, 1, 1)
            term = weight * weight_grad
            high = term.astype(LOW)
            rest = (term - high.astype(F32)).astype(LOW)
            inner = dot(high, ones, 1, 0) + dot(rest, ones, 1, 0)
            raw_grad = (weight * (weight_grad - inner) * damps[m, :, cols].astype(F32)).astype(LOW)
            key_part = from_head(dot(raw_grad, embed[m, :, cols], 0, 0))
            value_part = from_head(dot(weight.astype(LOW), mixed_grad, 0, 0))
            at = slice(j % 2 * GROUP, (j % 2 + 1) * GROUP)
            for p, part in ((j // 2, key_part), (2 + j // 2, value_part)):
                start = m * LAT_DEV
                halves[p, start : start + LAT_DEV, at] = part[:LAT_DEV].astype(LOW)
                start = start + HELD_ROWS
                halves[p, start : start + LAT_DEV, at] = part[LAT_DEV:].astype(LOW)
    for k, block in ((1, next1), (2, next2), (3, next3)):
        block[...] = halves[me[0] ^ k]


def latent_kernel(halves, key_weight, value_weight, own, upper):
    key_grad = jnp.concatenate([halves[0], halves[1]], axis=1)
    value_grad = jnp.concatenate([halves[2], halves[3]], axis=1)
    total = dot(key_grad, key_weight[...], 1, 1) + dot(value_grad, value_weight[...], 1, 1)
    own[...] = total[:HELD_ROWS]
    upper[...] = total[HELD_ROWS:].astype(LOW)


def weight_kernel(
    me, halves, last1, last2, last3, nodes, nodes1, nodes2, nodes3, shares, out_grad, upper, send
):
    rows = jnp.concatenate([halves[me[0]], last1[...], last2[...], last3[...]], axis=0)
    for j in range(GROUPS):
        cols = slice(j * GROUP, (j + 1) * GROUP)
        at = slice(j * HELD_ROWS, (j + 1) * HELD_ROWS)
        left = []
        for k, block in enumerate((nodes, nodes1, nodes2, nodes3)):
            left += [block[0, :, cols], block[1, :, cols], shares[me[0] ^ k, at]]
        left = jnp.concatenate(left, axis=0)
        product = dot(left, rows, 0, 0).astype(LOW)
        for b in range(GROUP // SHARE):
            r = j * (GROUP // SHARE) + b
            far, near = r // NEAR, r % NEAR
            at = slice(far * SHARE, (far + 1) * SHARE)
            send[near, at, :COLS] = product[b * SHARE : (b + 1) * SHARE]
            send[near, at, COLS:] = out_grad[r * SHARE : (r + 1) * SHARE]


def sum_kernel(parts, total):
    value = parts[0].astype(F32)
    for p in range(1, parts.shape[0]):
        value = value + parts[p].astype(F32)
    total[...] = value.astype(LOW)


def finish_kernel(
    parts, own, lower, key_weight_grad, value_weight_grad, out_weight_grad, grad_latent
):
    for m in range(HELD):
        rows = slice(m * LAT_DEV, (m + 1) * LAT_DEV)
        grad_latent[m] = own[rows] + lower[rows].astype(F32)
    total = parts[0, :, COLS:].astype(F32)
    for e in range(1, ENS):
        total = total + parts[e, :, COLS:].astype(F32)
    out_weight_grad[...] = total[:, :VARS]
    for p in range(2):
        key_weight_grad[:, p * COLS : (p + 1) * COLS] = parts[p, :, :COLS].astype(F32)
        value_weight_grad[:, p * COLS : (p + 1) * COLS] = parts[2 + p, :, :COLS].astype(F32)


def whole(shape):
    return pl.BlockSpec(shape, lambda i: (0,) * len(shape))


def call(kernel, outs, scratch=(), specs=None, flops=10**8, bytes_accessed=4 * 10**6):
    def run(*operands):
        places = specs or {}
        return pl.pallas_call(
            kernel,
            grid=(1,),
            in_specs=[places.get(i, whole(value.shape)) for i, value in enumerate(operands)],
            out_specs=[whole(shape) for shape, _ in outs],
            out_shape=[jax.ShapeDtypeStruct(shape, kind) for shape, kind in outs],
            scratch_shapes=[pltpu.VMEM(shape, kind) for shape, kind in scratch],
            compiler_params=pltpu.CompilerParams(vmem_limit_bytes=40 * 2**20),
            cost_estimate=pl.CostEstimate(
                flops=flops, bytes_accessed=bytes_accessed, transcendentals=0
            ),
            name=kernel.__name__,
        )(*operands)

    return run


def band_shift(value, by):
    return lax.ppermute(value, BAND, [(i, i + by) for i in range(64) if 0 <= i + by < 64])


def ens_swap(value, k):
    return lax.ppermute(value, "ens", [(e, e ^ k) for e in range(ENS)])


def on_device(grid_embed, latent, key_weight, value_weight, out_weight, target, edges):
    out_rows = jnp.pad(out_weight, ((0, VARS_PAD - VARS), (0, 0)))
    upper_latent = band_shift(latent, -1)
    nodes1, nodes2 = ens_swap(latent, 1), ens_swap(latent, 2)
    nodes3 = ens_swap(nodes2, 1)
    halves_of_key = (key_weight[:, : D // 2], key_weight[:, D // 2 :])
    own_keys, count = call(own_kernel, [((HELD_ROWS, D), LOW), ((GRID_DEV, GROUP), F32)])(
        latent, edges, *halves_of_key
    )
    preds, share, normed_low, inverse, exps, damps, values = call(
        forward_kernel,
        [
            ((HELD, VARS_PAD, GRID_DEV), F32),
            ((PRED_ROW + VARS_PAD, GROUP), LOW),
            ((HELD, GRID_DEV, D), LOW),
            ((HELD, GRID_DEV, 128), F32),
            ((HELD, GRID_DEV, D), LOW),
            ((HELD, GRID_DEV, D), LOW),
            ((HELD * WINDOW, D), LOW),
        ],
        [((HELD * WINDOW, D), LOW), ((GRID_DEV, D), F32)],
    )(
        grid_embed, latent, upper_latent, *halves_of_key, value_weight, out_rows, own_keys, count
    )
    me = lax.axis_index("ens").reshape(1)
    shares = lax.all_gather(share, "ens", axis=0)
    block = (2 * HELD_ROWS, COLS)
    scalar = {0: pl.BlockSpec(memory_space=pltpu.SMEM)}
    halves, next1, next2, next3, out_grad = call(
        backward_kernel,
        [((ENS, *block), LOW)] + [(block, LOW)] * 3 + [((D, VARS_PAD), LOW)],
        [((GRID_DEV, D), F32), ((VARS_PAD, GRID_DEV), F32)],
        {**scalar, 5: pl.BlockSpec((ENS, VARS_PAD, GROUP), lambda i: (0, PRED_ROW // VARS_PAD, 0))},
    )(me, grid_embed, out_rows, target, preds, shares, normed_low, inverse, exps, damps, values)
    last1, last2, last3 = (ens_swap(v, k) for k, v in ((1, next1), (2, next2), (3, next3)))
    own, upper = call(latent_kernel, [((HELD_ROWS, D), F32), ((HELD_ROWS, D), LOW)])(
        halves, key_weight, value_weight
    )
    lower = band_shift(upper, 1)
    (send,) = call(
        weight_kernel,
        [((NEAR, FAR * SHARE, COLS + VARS_PAD), LOW)],
        specs={
            **scalar,
            9: pl.BlockSpec((ENS, PRED_ROW, GROUP), lambda i: (0, 0, 0)),
            11: pl.BlockSpec((16, 128), lambda i: (0, 0)),
        },
    )(
        me, halves, last1, last2, last3, latent, nodes1, nodes2, nodes3, shares, out_grad, upper
    )
    parts = lax.all_to_all(send, ("x", "y"), 0, 0, tiled=True)
    (total,) = call(sum_kernel, [((FAR * SHARE, COLS + VARS_PAD), LOW)])(parts)
    parts = lax.all_to_all(total.reshape(FAR, SHARE, COLS + VARS_PAD), "z", 0, 0, tiled=True)
    (total,) = call(sum_kernel, [((SHARE, COLS + VARS_PAD), LOW)])(parts)
    parts = lax.all_gather(total, "ens", axis=0)
    return tuple(
        call(
            finish_kernel,
            [((16, D), F32), ((16, D), F32), ((16, VARS), F32), ((HELD, LAT_DEV, D), F32)],
        )(parts, own, lower)
    )


def solution(mesh):
    wide = Mesh(mesh.devices.reshape(4, 8, 4, 2), ("ens", *BAND))
    in_specs = (
        P("ens", BAND, None),
        P("ens", BAND, None),
        P(),
        P(),
        P(),
        P(None, BAND),
        P(None, BAND),
    )
    out_specs = (P(BAND, None), P(BAND, None), P(BAND, None), P("ens", BAND, None))
    return jax.shard_map(
        on_device, mesh=wide, in_specs=in_specs, out_specs=out_specs, check_vma=False
    )
```

```python
import jax
import jax.numpy as jnp
from jax import lax
from jax.experimental import pallas as pl
from jax.experimental.pallas import tpu as pltpu
from jax.sharding import Mesh
from jax.sharding import PartitionSpec as P

HEAD_DIM = 64
CAP = 5.0
DELTA_SQ = 0.0625
EPS = 1e-06

MEMBERS = 8
HELD = 2
GRID_DEV = 128
LAT_DEV = 32
WINDOW = 64
D = 1024
VARS = 100
VARS_PAD = 128
GROUP = 256
GROUPS = D // GROUP
BAND = ("z", "x", "y")
ENS = 4
NEAR = 8
FAR = 8
SHARE = 16
COLS = 2 * D // ENS
HELD_ROWS = HELD * LAT_DEV
PRED_ROW = HELD_ROWS * GROUPS

F32 = jnp.float32
LOW = jnp.bfloat16


def slope(offset):
    return offset * lax.rsqrt(offset * offset + DELTA_SQ)


def dot(a, b, a_dim, b_dim):
    return lax.dot_general(a, b, (((a_dim,), (b_dim,)), ((), ())), preferred_element_type=F32)


def same_head():
    rows = lax.broadcasted_iota(jnp.int32, (GROUP, GROUP), 0) // HEAD_DIM
    cols = lax.broadcasted_iota(jnp.int32, (GROUP, GROUP), 1) // HEAD_DIM
    return rows == cols


def by_head(rows, same):
    return jnp.where(same, jnp.concatenate([rows] * 4, axis=0), jnp.zeros((), LOW))


def head_sums(values):
    heads = values.reshape(GROUP // WINDOW, WINDOW, GRID_DEV)
    return heads, jnp.sum(heads, axis=1, keepdims=True)


def shares_of(exp):
    heads, totals = head_sums(exp.astype(F32))
    return (heads * (1.0 / totals)).reshape(GROUP, GRID_DEV)


def from_head(blocks):
    head = lax.broadcasted_iota(jnp.int32, (WINDOW, GROUP), 1) // HEAD_DIM
    total = blocks[:WINDOW]
    for h in range(1, 4):
        total = jnp.where(head == h, blocks[h * WINDOW : (h + 1) * WINDOW], total)
    return total


def own_kernel(latent, edges, key_left, key_right, keys, count):
    rows = jnp.concatenate([latent[0], latent[1]], axis=0)
    keys[:, : D // 2] = dot(rows, key_left[...], 1, 0).astype(LOW)
    keys[:, D // 2 :] = dot(rows, key_right[...], 1, 0).astype(LOW)
    target = edges[0:1, :]
    local = jnp.where(target >= 0, target & (GRID_DEV - 1), -1)
    source = edges[1:2, :] - (target >> 7) * LAT_DEV
    slots = edges.shape[1]
    into = (lax.broadcasted_iota(jnp.int32, (GRID_DEV, slots), 0) == local).astype(F32).astype(LOW)
    node = lax.broadcasted_iota(jnp.int32, (GROUP, slots), 0) & (WINDOW - 1)
    out_of = (node == source).astype(F32).astype(LOW)
    count[...] = dot(out_of, into, 1, 1)


def forward_kernel(
    embed, latent, lat_up, key_left, key_right, value_weight, out_weight, own_keys, edge_count,
    preds, share, normed_low, inverse, exps, damps, values,
    keys, mixed,
):
    rows = jnp.concatenate([latent[0], lat_up[0], latent[1], lat_up[1]], axis=0)
    values[...] = dot(rows, value_weight[...], 1, 0).astype(LOW)
    rows = jnp.concatenate([lat_up[0], lat_up[1]], axis=0)
    for c, weight in enumerate((key_left, key_right)):
        cols = slice(c * (D // 2), (c + 1) * (D // 2))
        upper_rows = dot(rows, weight[...], 1, 0).astype(LOW)
        for m in range(HELD):
            part = slice(m * LAT_DEV, (m + 1) * LAT_DEV)
            keys[m * WINDOW : m * WINDOW + LAT_DEV, cols] = own_keys[part, cols]
            keys[m * WINDOW + LAT_DEV : (m + 1) * WINDOW, cols] = upper_rows[part]
    count = edge_count[...]
    same = same_head()
    rows = lax.broadcasted_iota(jnp.int32, (GRID_DEV, GRID_DEV), 0)
    cols = lax.broadcasted_iota(jnp.int32, (GRID_DEV, GRID_DEV), 1)
    identity = (rows == cols).astype(F32).astype(LOW)
    for m in range(HELD):
        square = jnp.zeros((GRID_DEV, 1), F32)
        for j in range(GROUPS):
            cols = slice(j * GROUP, (j + 1) * GROUP)
            start = j * HELD_ROWS + m * LAT_DEV
            share[start : start + LAT_DEV] = lat_up[m, :, cols]
            query = embed[m, :, cols]
            key = by_head(keys[m * WINDOW : (m + 1) * WINDOW, cols], same)
            value = by_head(values[m * WINDOW : (m + 1) * WINDOW, cols], same)
            bent = jnp.tanh(dot(key, query, 1, 1) * (HEAD_DIM**-0.5 / CAP))
            exp = (count * jnp.exp(CAP * bent)).astype(LOW)
            exps[m, j] = exp
            damps[m, j] = ((1.0 - bent * bent) * HEAD_DIM**-0.5).astype(LOW)
            turned = dot(identity, shares_of(exp).astype(LOW), 1, 1).astype(LOW)
            attended = dot(turned, value, 1, 0)
            sums = query.astype(F32) + attended
            mixed[:, cols] = sums
            square = square + jnp.sum(sums * sums, axis=1, keepdims=True)
        inv = lax.rsqrt(square * (1.0 / D) + EPS)
        low = (mixed[...] * inv).astype(LOW)
        normed_low[m] = low
        inverse[m] = jnp.broadcast_to(inv, (GRID_DEV, 128))
        pred = dot(out_weight[...], low, 1, 1)
        preds[m] = pred
        share[PRED_ROW:, m * GRID_DEV : (m + 1) * GRID_DEV] = pred.astype(LOW)


def backward_kernel(
    me, embed, out_weight, target, preds, every, normed_low, inverse, exps, damps, values,
    halves, next1, next2, next3, out_grad,
    grad, truth,
):
    truth[...] = jnp.zeros((VARS_PAD, GRID_DEV), F32)
    truth[:VARS, :] = target[...]
    same = same_head()
    pred_grads = []
    for m in range(HELD):
        pred = preds[m]
        pair = jnp.zeros((VARS_PAD, GRID_DEV), F32)
        for e in range(MEMBERS // HELD):
            for k in range(HELD):
                pair = pair + slope(pred - every[e, :, k * GRID_DEV : (k + 1) * GRID_DEV].astype(F32))
        for k in range(HELD):
            pair = pair - slope(pred - preds[k].astype(LOW).astype(F32))
            if k != m:
                pair = pair + slope(pred - preds[k])
        base = slope(pred - truth[...]) * (1.0 / MEMBERS)
        pred_grads.append((base - pair * (1.0 / (MEMBERS * (MEMBERS - 1)))).astype(LOW))
    both = jnp.concatenate(pred_grads, axis=1)
    lows = jnp.concatenate([normed_low[0], normed_low[1]], axis=0)
    out_grad[...] = jnp.transpose(dot(both, lows, 1, 0)).astype(LOW)
    for m in range(HELD):
        slant = jnp.zeros((GRID_DEV, 1), F32)
        turned = jnp.transpose(pred_grads[m].astype(F32)).astype(LOW)
        for j in range(GROUPS):
            cols = slice(j * GROUP, (j + 1) * GROUP)
            part = dot(turned, out_weight[:, cols], 1, 0)
            grad[:, cols] = part
            slant = slant + jnp.sum(part * normed_low[m, :, cols].astype(F32), axis=1, keepdims=True)
        slant = slant * (1.0 / D)
        inv = inverse[m][:, :1]
        for j in range(GROUPS):
            cols = slice(j * GROUP, (j + 1) * GROUP)
            mixed_grad = (inv * (grad[:, cols] - normed_low[m, :, cols].astype(F32) * slant)).astype(LOW)
            value = by_head(values[m * WINDOW : (m + 1) * WINDOW, cols], same)
            weight = shares_of(exps[m, j])
            weight_grad = dot(value, mixed_grad, 1, 1)
            inner = head_sums(weight * weight_grad)[1]
            centred = weight_grad.reshape(GROUP // WINDOW, WINDOW, GRID_DEV) - inner
            raw_grad = weight * centred.reshape(GROUP, GRID_DEV) * damps[m, j].astype(F32)
            key_part = from_head(dot(raw_grad.astype(LOW), embed[m, :, cols], 1, 0))
            value_part = from_head(dot(weight.astype(LOW), mixed_grad, 1, 0))
            at = slice(j % 2 * GROUP, (j % 2 + 1) * GROUP)
            for p, part in ((j // 2, key_part), (2 + j // 2, value_part)):
                start = m * LAT_DEV
                halves[p, start : start + LAT_DEV, at] = part[:LAT_DEV].astype(LOW)
                start = start + HELD_ROWS
                halves[p, start : start + LAT_DEV, at] = part[LAT_DEV:].astype(LOW)
    for k, block in ((1, next1), (2, next2), (3, next3)):
        block[: 2 * HELD_ROWS] = halves[me[0] ^ k]
    for f in range(FAR // 2):
        start = pl.multiple_of(((me[0] & 1) ^ 1) * (D // 2) + f * NEAR * SHARE, NEAR * SHARE)
        next1[2 * HELD_ROWS :, f * VARS_PAD : (f + 1) * VARS_PAD] = out_grad[
            pl.ds(start, NEAR * SHARE), :
        ]


def latent_kernel(halves, key_weight, value_weight, own, upper):
    key_grad = jnp.concatenate([halves[0], halves[1]], axis=1)
    value_grad = jnp.concatenate([halves[2], halves[3]], axis=1)
    total = dot(key_grad, key_weight[...], 1, 1) + dot(value_grad, value_weight[...], 1, 1)
    own[...] = total[:HELD_ROWS]
    upper[...] = total[HELD_ROWS:].astype(LOW)


def weight_kernel(
    me, halves, last1, last2, last3, nodes, nodes1, nodes2, nodes3, shares, out_grad, upper, send
):
    rows = jnp.concatenate(
        [halves[me[0]], last1[: 2 * HELD_ROWS], last2[...], last3[...]], axis=0
    )
    for j in range(GROUPS):
        cols = slice(j * GROUP, (j + 1) * GROUP)
        at = slice(j * HELD_ROWS, (j + 1) * HELD_ROWS)
        left = []
        for k, block in enumerate((nodes, nodes1, nodes2, nodes3)):
            left += [block[0, :, cols], block[1, :, cols], shares[me[0] ^ k, at]]
        left = jnp.concatenate(left, axis=0)
        product = dot(left, rows, 0, 0).astype(LOW)
        for b in range(GROUP // SHARE):
            r = j * (GROUP // SHARE) + b
            far, near = r // NEAR, r % NEAR
            at = slice(far * SHARE, (far + 1) * SHARE)
            send[near, at] = product[b * SHARE : (b + 1) * SHARE]
    for f in range(FAR // 2):
        start = pl.multiple_of((me[0] & 1) * (D // 2) + f * NEAR * SHARE, NEAR * SHARE)
        cols = slice(f * VARS_PAD, (f + 1) * VARS_PAD)
        pair = out_grad[pl.ds(start, NEAR * SHARE), :].astype(F32)
        pair = (pair + last1[2 * HELD_ROWS :, cols].astype(F32)).astype(LOW)
        for near in range(NEAR):
            send[near, FAR * SHARE :, cols] = pair[near * SHARE : (near + 1) * SHARE]


def near_sum_kernel(me, parts, total):
    value = parts[0].astype(F32)
    for p in range(1, NEAR):
        value = value + parts[p].astype(F32)
    for far in range(FAR):
        total[far, :, :COLS] = value[far * SHARE : (far + 1) * SHARE].astype(LOW)
        f = far % (FAR // 2)
        held = jnp.where((me[0] & 1) == far // (FAR // 2), 1.0, 0.0)
        block = value[FAR * SHARE :, f * VARS_PAD : (f + 1) * VARS_PAD]
        total[far, :, COLS:] = (block * held).astype(LOW)


def sum_kernel(parts, total):
    value = parts[0].astype(F32)
    for p in range(1, parts.shape[0]):
        value = value + parts[p].astype(F32)
    total[...] = value.astype(LOW)


def finish_kernel(
    parts, own, lower, key_weight_grad, value_weight_grad, out_weight_grad, grad_latent
):
    for m in range(HELD):
        rows = slice(m * LAT_DEV, (m + 1) * LAT_DEV)
        grad_latent[m] = own[rows] + lower[rows].astype(F32)
    total = parts[0, :, COLS:].astype(F32)
    for e in range(1, ENS):
        total = total + parts[e, :, COLS:].astype(F32)
    out_weight_grad[...] = total[:, :VARS]
    for p in range(2):
        key_weight_grad[:, p * COLS : (p + 1) * COLS] = parts[p, :, :COLS].astype(F32)
        value_weight_grad[:, p * COLS : (p + 1) * COLS] = parts[2 + p, :, :COLS].astype(F32)


def whole(shape):
    return pl.BlockSpec(shape, lambda i: (0,) * len(shape))


def call(kernel, outs, scratch=(), specs=None, flops=10**8, bytes_accessed=4 * 10**6):
    def run(*operands):
        places = specs or {}
        return pl.pallas_call(
            kernel,
            grid=(1,),
            in_specs=[places.get(i, whole(value.shape)) for i, value in enumerate(operands)],
            out_specs=[whole(shape) for shape, _ in outs],
            out_shape=[jax.ShapeDtypeStruct(shape, kind) for shape, kind in outs],
            scratch_shapes=[pltpu.VMEM(shape, kind) for shape, kind in scratch],
            compiler_params=pltpu.CompilerParams(vmem_limit_bytes=40 * 2**20),
            cost_estimate=pl.CostEstimate(
                flops=flops, bytes_accessed=bytes_accessed, transcendentals=0
            ),
            name=kernel.__name__,
        )(*operands)

    return run


def band_shift(value, by):
    return lax.ppermute(value, BAND, [(i, i + by) for i in range(64) if 0 <= i + by < 64])


def ens_swap(value, k):
    return lax.ppermute(value, "ens", [(e, e ^ k) for e in range(ENS)])


def on_device(grid_embed, latent, key_weight, value_weight, out_weight, target, edges):
    out_rows = jnp.pad(out_weight, ((0, VARS_PAD - VARS), (0, 0)))
    upper_latent = band_shift(latent, -1)
    nodes1, nodes2 = ens_swap(latent, 1), ens_swap(latent, 2)
    nodes3 = ens_swap(nodes2, 1)
    halves_of_key = (key_weight[:, : D // 2], key_weight[:, D // 2 :])
    own_keys, count = call(own_kernel, [((HELD_ROWS, D), LOW), ((GROUP, GRID_DEV), F32)])(
        latent, edges, *halves_of_key
    )
    preds, share, normed_low, inverse, exps, damps, values = call(
        forward_kernel,
        [
            ((HELD, VARS_PAD, GRID_DEV), F32),
            ((PRED_ROW + VARS_PAD, GROUP), LOW),
            ((HELD, GRID_DEV, D), LOW),
            ((HELD, GRID_DEV, 128), F32),
            ((HELD, GROUPS, GROUP, GRID_DEV), LOW),
            ((HELD, GROUPS, GROUP, GRID_DEV), LOW),
            ((HELD * WINDOW, D), LOW),
        ],
        [((HELD * WINDOW, D), LOW), ((GRID_DEV, D), F32)],
    )(
        grid_embed, latent, upper_latent, *halves_of_key, value_weight, out_rows, own_keys, count
    )
    me = lax.axis_index("ens").reshape(1)
    shares = lax.all_gather(share, "ens", axis=0)
    block = (2 * HELD_ROWS, COLS)
    scalar = {0: pl.BlockSpec(memory_space=pltpu.SMEM)}
    halves, next1, next2, next3, out_grad = call(
        backward_kernel,
        [((ENS, *block), LOW), ((2 * HELD_ROWS + NEAR * SHARE, COLS), LOW)]
        + [(block, LOW)] * 2
        + [((D, VARS_PAD), LOW)],
        [((GRID_DEV, D), F32), ((VARS_PAD, GRID_DEV), F32)],
        {**scalar, 5: pl.BlockSpec((ENS, VARS_PAD, GROUP), lambda i: (0, PRED_ROW // VARS_PAD, 0))},
    )(me, grid_embed, out_rows, target, preds, shares, normed_low, inverse, exps, damps, values)
    last1, last2, last3 = (ens_swap(v, k) for k, v in ((1, next1), (2, next2), (3, next3)))
    own, upper = call(latent_kernel, [((HELD_ROWS, D), F32), ((HELD_ROWS, D), LOW)])(
        halves, key_weight, value_weight
    )
    lower = band_shift(upper, 1)
    (send,) = call(
        weight_kernel,
        [((NEAR, (FAR + 1) * SHARE, COLS), LOW)],
        specs={
            **scalar,
            9: pl.BlockSpec((ENS, PRED_ROW, GROUP), lambda i: (0, 0, 0)),
            11: pl.BlockSpec((16, 128), lambda i: (0, 0)),
        },
    )(
        me, halves, last1, last2, last3, latent, nodes1, nodes2, nodes3, shares, out_grad, upper
    )
    parts = lax.all_to_all(send, ("x", "y"), 0, 0, tiled=True)
    (total,) = call(near_sum_kernel, [((FAR, SHARE, COLS + VARS_PAD), LOW)], specs=scalar)(me, parts)
    parts = lax.all_to_all(total, "z", 0, 0, tiled=True)
    (total,) = call(sum_kernel, [((SHARE, COLS + VARS_PAD), LOW)])(parts)
    parts = lax.all_gather(total, "ens", axis=0)
    return tuple(
        call(
            finish_kernel,
            [((16, D), F32), ((16, D), F32), ((16, VARS), F32), ((HELD, LAT_DEV, D), F32)],
        )(parts, own, lower)
    )


def solution(mesh):
    wide = Mesh(mesh.devices.reshape(4, 8, 4, 2), ("ens", *BAND))
    in_specs = (
        P("ens", BAND, None),
        P("ens", BAND, None),
        P(),
        P(),
        P(),
        P(None, BAND),
        P(None, BAND),
    )
    out_specs = (P(BAND, None), P(BAND, None), P(BAND, None), P("ens", BAND, None))
    return jax.shard_map(
        on_device, mesh=wide, in_specs=in_specs, out_specs=out_specs, check_vma=False
    )
```

```python
import jax
import jax.numpy as jnp
from jax import lax
from jax.experimental import pallas as pl
from jax.experimental.pallas import tpu as pltpu
from jax.sharding import Mesh
from jax.sharding import PartitionSpec as P

HEAD_DIM = 64
CAP = 5.0
DELTA_SQ = 0.0625
EPS = 1e-06

MEMBERS = 8
HELD = 2
GRID_DEV = 128
LAT_DEV = 32
WINDOW = 64
D = 1024
VARS = 100
VARS_PAD = 128
GROUP = 256
GROUPS = D // GROUP
BAND = ("z", "x", "y")
ENS = 4
NEAR = 8
STEPS = ((2, 0), (2, 1), (0, 1), (1, 1), (3, 0), (1, 0), (3, 1))
PATHS = ((1, 0), (3, 0), (0, 1), (1, 1), (3, 0), (1, 0), (3, 1))
FAR = 8
SHARE = 16
COLS = 2 * D // ENS
HELD_ROWS = HELD * LAT_DEV
PRED_ROW = HELD_ROWS * GROUPS

F32 = jnp.float32
LOW = jnp.bfloat16


def slope(offset):
    return offset * lax.rsqrt(offset * offset + DELTA_SQ)


def dot(a, b, a_dim, b_dim):
    return lax.dot_general(a, b, (((a_dim,), (b_dim,)), ((), ())), preferred_element_type=F32)


def same_head():
    rows = lax.broadcasted_iota(jnp.int32, (GROUP, GROUP), 0) // HEAD_DIM
    cols = lax.broadcasted_iota(jnp.int32, (GROUP, GROUP), 1) // HEAD_DIM
    return rows == cols


def by_head(rows, same):
    return jnp.where(same, jnp.concatenate([rows] * 4, axis=0), jnp.zeros((), LOW))


def head_sums(values):
    heads = values.reshape(GROUP // WINDOW, WINDOW, GRID_DEV)
    return heads, jnp.sum(heads, axis=1, keepdims=True)


def shares_of(exp):
    heads, totals = head_sums(exp.astype(F32))
    return (heads * (1.0 / totals)).reshape(GROUP, GRID_DEV)


def from_head(blocks):
    head = lax.broadcasted_iota(jnp.int32, (WINDOW, GROUP), 1) // HEAD_DIM
    total = blocks[:WINDOW]
    for h in range(1, 4):
        total = jnp.where(head == h, blocks[h * WINDOW : (h + 1) * WINDOW], total)
    return total


def own_kernel(latent, edges, key_left, key_right, keys, count):
    rows = jnp.concatenate([latent[0], latent[1]], axis=0)
    keys[:, : D // 2] = dot(rows, key_left[...], 1, 0).astype(LOW)
    keys[:, D // 2 :] = dot(rows, key_right[...], 1, 0).astype(LOW)
    target = edges[0:1, :]
    local = jnp.where(target >= 0, target & (GRID_DEV - 1), -1)
    source = edges[1:2, :] - (target >> 7) * LAT_DEV
    slots = edges.shape[1]
    into = (lax.broadcasted_iota(jnp.int32, (GRID_DEV, slots), 0) == local).astype(F32).astype(LOW)
    node = lax.broadcasted_iota(jnp.int32, (GROUP, slots), 0) & (WINDOW - 1)
    out_of = (node == source).astype(F32).astype(LOW)
    count[...] = dot(out_of, into, 1, 1)


def forward_kernel(
    embed, latent, lat_up, key_left, key_right, value_weight, out_weight, own_keys, edge_count,
    preds, share, normed_low, inverse, exps, damps, values,
    keys, mixed,
):
    rows = jnp.concatenate([latent[0], lat_up[0], latent[1], lat_up[1]], axis=0)
    values[...] = dot(rows, value_weight[...], 1, 0).astype(LOW)
    rows = jnp.concatenate([lat_up[0], lat_up[1]], axis=0)
    for c, weight in enumerate((key_left, key_right)):
        cols = slice(c * (D // 2), (c + 1) * (D // 2))
        upper_rows = dot(rows, weight[...], 1, 0).astype(LOW)
        for m in range(HELD):
            part = slice(m * LAT_DEV, (m + 1) * LAT_DEV)
            keys[m * WINDOW : m * WINDOW + LAT_DEV, cols] = own_keys[part, cols]
            keys[m * WINDOW + LAT_DEV : (m + 1) * WINDOW, cols] = upper_rows[part]
    count = edge_count[...]
    same = same_head()
    rows = lax.broadcasted_iota(jnp.int32, (GRID_DEV, GRID_DEV), 0)
    cols = lax.broadcasted_iota(jnp.int32, (GRID_DEV, GRID_DEV), 1)
    identity = (rows == cols).astype(F32).astype(LOW)
    for m in range(HELD):
        square = jnp.zeros((GRID_DEV, 1), F32)
        for j in range(GROUPS):
            cols = slice(j * GROUP, (j + 1) * GROUP)
            start = j * HELD_ROWS + m * LAT_DEV
            share[start : start + LAT_DEV] = lat_up[m, :, cols]
            query = embed[m, :, cols]
            key = by_head(keys[m * WINDOW : (m + 1) * WINDOW, cols], same)
            value = by_head(values[m * WINDOW : (m + 1) * WINDOW, cols], same)
            bent = jnp.tanh(dot(key, query, 1, 1) * (HEAD_DIM**-0.5 / CAP))
            exp = (count * jnp.exp(CAP * bent)).astype(LOW)
            exps[m, j] = exp
            damps[m, j] = ((1.0 - bent * bent) * HEAD_DIM**-0.5).astype(LOW)
            turned = dot(identity, shares_of(exp).astype(LOW), 1, 1).astype(LOW)
            attended = dot(turned, value, 1, 0)
            sums = query.astype(F32) + attended
            mixed[:, cols] = sums
            square = square + jnp.sum(sums * sums, axis=1, keepdims=True)
        inv = lax.rsqrt(square * (1.0 / D) + EPS)
        low = (mixed[...] * inv).astype(LOW)
        normed_low[m] = low
        inverse[m] = jnp.broadcast_to(inv, (GRID_DEV, 128))
        pred = dot(out_weight[...], low, 1, 1)
        preds[m] = pred
        share[PRED_ROW:, m * GRID_DEV : (m + 1) * GRID_DEV] = pred.astype(LOW)


def backward_kernel(
    me, embed, out_weight, target, preds, every, normed_low, inverse, exps, damps, values,
    halves, next1, next2, next3, out_grad,
    grad, truth,
):
    truth[...] = jnp.zeros((VARS_PAD, GRID_DEV), F32)
    truth[:VARS, :] = target[...]
    same = same_head()
    pred_grads = []
    for m in range(HELD):
        pred = preds[m]
        pair = jnp.zeros((VARS_PAD, GRID_DEV), F32)
        for e in range(MEMBERS // HELD):
            for k in range(HELD):
                pair = pair + slope(pred - every[e, :, k * GRID_DEV : (k + 1) * GRID_DEV].astype(F32))
        for k in range(HELD):
            pair = pair - slope(pred - preds[k].astype(LOW).astype(F32))
            if k != m:
                pair = pair + slope(pred - preds[k])
        base = slope(pred - truth[...]) * (1.0 / MEMBERS)
        pred_grads.append((base - pair * (1.0 / (MEMBERS * (MEMBERS - 1)))).astype(LOW))
    both = jnp.concatenate(pred_grads, axis=1)
    lows = jnp.concatenate([normed_low[0], normed_low[1]], axis=0)
    out_grad[...] = jnp.transpose(dot(both, lows, 1, 0)).astype(LOW)
    for m in range(HELD):
        slant = jnp.zeros((GRID_DEV, 1), F32)
        turned = jnp.transpose(pred_grads[m].astype(F32)).astype(LOW)
        for j in range(GROUPS):
            cols = slice(j * GROUP, (j + 1) * GROUP)
            part = dot(turned, out_weight[:, cols], 1, 0)
            grad[:, cols] = part
            slant = slant + jnp.sum(part * normed_low[m, :, cols].astype(F32), axis=1, keepdims=True)
        slant = slant * (1.0 / D)
        inv = inverse[m][:, :1]
        for j in range(GROUPS):
            cols = slice(j * GROUP, (j + 1) * GROUP)
            mixed_grad = (inv * (grad[:, cols] - normed_low[m, :, cols].astype(F32) * slant)).astype(LOW)
            value = by_head(values[m * WINDOW : (m + 1) * WINDOW, cols], same)
            weight = shares_of(exps[m, j])
            weight_grad = dot(value, mixed_grad, 1, 1)
            inner = head_sums(weight * weight_grad)[1]
            centred = weight_grad.reshape(GROUP // WINDOW, WINDOW, GRID_DEV) - inner
            raw_grad = weight * centred.reshape(GROUP, GRID_DEV) * damps[m, j].astype(F32)
            key_part = from_head(dot(raw_grad.astype(LOW), embed[m, :, cols], 1, 0))
            value_part = from_head(dot(weight.astype(LOW), mixed_grad, 1, 0))
            at = slice(j % 2 * GROUP, (j % 2 + 1) * GROUP)
            for p, part in ((j // 2, key_part), (2 + j // 2, value_part)):
                start = m * LAT_DEV
                halves[p, start : start + LAT_DEV, at] = part[:LAT_DEV].astype(LOW)
                start = start + HELD_ROWS
                halves[p, start : start + LAT_DEV, at] = part[LAT_DEV:].astype(LOW)
    for k, block in ((1, next1), (2, next2), (3, next3)):
        block[: 2 * HELD_ROWS] = halves[(me[0] & (ENS - 1)) ^ k]
    for f in range(FAR // 2):
        start = pl.multiple_of(((me[0] & 1) ^ 1) * (D // 2) + f * NEAR * SHARE, NEAR * SHARE)
        next1[2 * HELD_ROWS :, f * VARS_PAD : (f + 1) * VARS_PAD] = out_grad[
            pl.ds(start, NEAR * SHARE), :
        ]


def latent_kernel(halves, key_weight, value_weight, own, upper):
    key_grad = jnp.concatenate([halves[0], halves[1]], axis=1)
    value_grad = jnp.concatenate([halves[2], halves[3]], axis=1)
    total = dot(key_grad, key_weight[...], 1, 1) + dot(value_grad, value_weight[...], 1, 1)
    own[...] = total[:HELD_ROWS]
    upper[...] = total[HELD_ROWS:].astype(LOW)


def weight_kernel(
    me, halves, last1, last2, last3, nodes, nodes1, nodes2, nodes3, shares, out_grad,
    upper, keep, *refs,
):
    sends, product, pair = refs[: NEAR - 1], refs[-2], refs[-1]
    rows = jnp.concatenate(
        [halves[me[0] & (ENS - 1)], last1[: 2 * HELD_ROWS], last2[...], last3[...]], axis=0
    )
    for j in range(GROUPS):
        cols = slice(j * GROUP, (j + 1) * GROUP)
        at = slice(j * HELD_ROWS, (j + 1) * HELD_ROWS)
        left = []
        for k, block in enumerate((nodes, nodes1, nodes2, nodes3)):
            left += [block[0, :, cols], block[1, :, cols], shares[(me[0] & (ENS - 1)) ^ k, at]]
        left = jnp.concatenate(left, axis=0)
        product[cols, :] = dot(left, rows, 0, 0).astype(LOW)
    for f in range(FAR // 2):
        start = pl.multiple_of((me[0] & 1) * (D // 2) + f * NEAR * SHARE, NEAR * SHARE)
        lanes = slice(f * VARS_PAD, (f + 1) * VARS_PAD)
        own = out_grad[pl.ds(start, NEAR * SHARE), :].astype(F32)
        pair[:, lanes] = (own + last1[2 * HELD_ROWS :, lanes].astype(F32)).astype(LOW)
    for (dx, dy), send in zip(((0, 0), *STEPS), (keep, *sends)):
        near = (((me[0] >> 3) + dx) & 3) * 2 + (((me[0] >> 2) + dy) & 1)
        for far in range(FAR):
            start = pl.multiple_of((far * NEAR + near) * SHARE, SHARE)
            send[far * SHARE : (far + 1) * SHARE] = product[pl.ds(start, SHARE), :]
        start = pl.multiple_of(near * SHARE, SHARE)
        send[FAR * SHARE :] = pair[pl.ds(start, SHARE), :]


def relay_kernel(up, down, held6, held7, send6, send7):
    send6[...] = (held6[...].astype(F32) + up[...].astype(F32)).astype(LOW)
    send7[...] = (held7[...].astype(F32) + down[...].astype(F32)).astype(LOW)


def near_sum_kernel(me, first, *refs):
    value, total = first[...].astype(F32), refs[-1]
    for part in refs[:-1]:
        value = value + part[...].astype(F32)
    for far in range(FAR):
        total[far, :, :COLS] = value[far * SHARE : (far + 1) * SHARE].astype(LOW)
        f = far % (FAR // 2)
        held = jnp.where((me[0] & 1) == far // (FAR // 2), 1.0, 0.0)
        block = value[FAR * SHARE :, f * VARS_PAD : (f + 1) * VARS_PAD]
        total[far, :, COLS:] = (block * held).astype(LOW)


def sum_kernel(parts, total):
    value = parts[0].astype(F32)
    for p in range(1, parts.shape[0]):
        value = value + parts[p].astype(F32)
    total[...] = value.astype(LOW)


def finish_kernel(
    parts, own, lower, key_weight_grad, value_weight_grad, out_weight_grad, grad_latent
):
    for m in range(HELD):
        rows = slice(m * LAT_DEV, (m + 1) * LAT_DEV)
        grad_latent[m] = own[rows] + lower[rows].astype(F32)
    total = parts[0, :, COLS:].astype(F32)
    for e in range(1, ENS):
        total = total + parts[e, :, COLS:].astype(F32)
    out_weight_grad[...] = total[:, :VARS]
    for p in range(2):
        key_weight_grad[:, p * COLS : (p + 1) * COLS] = parts[p, :, :COLS].astype(F32)
        value_weight_grad[:, p * COLS : (p + 1) * COLS] = parts[2 + p, :, :COLS].astype(F32)


def whole(shape):
    return pl.BlockSpec(shape, lambda i: (0,) * len(shape))


def call(kernel, outs, scratch=(), specs=None, flops=10**8, bytes_accessed=4 * 10**6):
    def run(*operands):
        places = specs or {}
        return pl.pallas_call(
            kernel,
            grid=(1,),
            in_specs=[places.get(i, whole(value.shape)) for i, value in enumerate(operands)],
            out_specs=[whole(shape) for shape, _ in outs],
            out_shape=[jax.ShapeDtypeStruct(shape, kind) for shape, kind in outs],
            scratch_shapes=[pltpu.VMEM(shape, kind) for shape, kind in scratch],
            compiler_params=pltpu.CompilerParams(vmem_limit_bytes=40 * 2**20),
            cost_estimate=pl.CostEstimate(
                flops=flops, bytes_accessed=bytes_accessed, transcendentals=0
            ),
            name=kernel.__name__,
        )(*operands)

    return run


def band_shift(value, by):
    return lax.ppermute(value, BAND, [(i, i + by) for i in range(64) if 0 <= i + by < 64])


def ens_swap(value, k):
    return lax.ppermute(value, "ens", [(e, e ^ k) for e in range(ENS)])


def near_shift(value, dx, dy):
    pairs = [(x * 2 + y, (x + dx) % 4 * 2 + (y + dy) % 2) for x in range(4) for y in range(2)]
    return lax.ppermute(value, ("x", "y"), pairs)


def on_device(grid_embed, latent, key_weight, value_weight, out_weight, target, edges):
    out_rows = jnp.pad(out_weight, ((0, VARS_PAD - VARS), (0, 0)))
    upper_latent = band_shift(latent, -1)
    nodes1, nodes2 = ens_swap(latent, 1), ens_swap(latent, 2)
    nodes3 = ens_swap(nodes2, 1)
    halves_of_key = (key_weight[:, : D // 2], key_weight[:, D // 2 :])
    own_keys, count = call(own_kernel, [((HELD_ROWS, D), LOW), ((GROUP, GRID_DEV), F32)])(
        latent, edges, *halves_of_key
    )
    preds, share, normed_low, inverse, exps, damps, values = call(
        forward_kernel,
        [
            ((HELD, VARS_PAD, GRID_DEV), F32),
            ((PRED_ROW + VARS_PAD, GROUP), LOW),
            ((HELD, GRID_DEV, D), LOW),
            ((HELD, GRID_DEV, 128), F32),
            ((HELD, GROUPS, GROUP, GRID_DEV), LOW),
            ((HELD, GROUPS, GROUP, GRID_DEV), LOW),
            ((HELD * WINDOW, D), LOW),
        ],
        [((HELD * WINDOW, D), LOW), ((GRID_DEV, D), F32)],
    )(
        grid_embed, latent, upper_latent, *halves_of_key, value_weight, out_rows, own_keys, count
    )
    spot = (lax.axis_index("x") * 2 + lax.axis_index("y")) * ENS + lax.axis_index("ens")
    me = spot.reshape(1)
    shares = lax.all_gather(share, "ens", axis=0)
    block = (2 * HELD_ROWS, COLS)
    scalar = {0: pl.BlockSpec(memory_space=pltpu.SMEM)}
    halves, next1, next2, next3, out_grad = call(
        backward_kernel,
        [((ENS, *block), LOW), ((2 * HELD_ROWS + NEAR * SHARE, COLS), LOW)]
        + [(block, LOW)] * 2
        + [((D, VARS_PAD), LOW)],
        [((GRID_DEV, D), F32), ((VARS_PAD, GRID_DEV), F32)],
        {**scalar, 5: pl.BlockSpec((ENS, VARS_PAD, GROUP), lambda i: (0, PRED_ROW // VARS_PAD, 0))},
    )(me, grid_embed, out_rows, target, preds, shares, normed_low, inverse, exps, damps, values)
    last1, last2, last3 = (ens_swap(v, k) for k, v in ((1, next1), (2, next2), (3, next3)))
    own, upper = call(latent_kernel, [((HELD_ROWS, D), F32), ((HELD_ROWS, D), LOW)])(
        halves, key_weight, value_weight
    )
    lower = band_shift(upper, 1)
    share_block = ((FAR + 1) * SHARE, COLS)
    keep, *sends = call(
        weight_kernel,
        [(share_block, LOW)] * NEAR,
        [((D, COLS), LOW), ((NEAR * SHARE, COLS), LOW)],
        specs={
            **{i: pl.BlockSpec(memory_space=pltpu.SMEM) for i in range(1)},
            9: pl.BlockSpec((ENS, PRED_ROW, GROUP), lambda i: (0, 0, 0)),
            11: pl.BlockSpec((16, 128), lambda i: (0, 0)),
        },
    )(
        me, halves, last1, last2, last3, latent, nodes1, nodes2, nodes3, shares,
        out_grad, upper,
    )
    parts = [near_shift(value, *step) for step, value in zip(PATHS[:5], sends[:5])]
    relayed = call(relay_kernel, [(share_block, LOW), (share_block, LOW)])(
        parts[0], parts[1], sends[5], sends[6]
    )
    parts = parts[2:] + [near_shift(value, *step) for step, value in zip(PATHS[5:], relayed)]
    (total,) = call(near_sum_kernel, [((FAR, SHARE, COLS + VARS_PAD), LOW)], specs=scalar)(
        me, keep, *parts
    )
    parts = lax.all_to_all(total, "z", 0, 0, tiled=True)
    (total,) = call(sum_kernel, [((SHARE, COLS + VARS_PAD), LOW)])(parts)
    parts = lax.all_gather(total, "ens", axis=0)
    return tuple(
        call(
            finish_kernel,
            [((16, D), F32), ((16, D), F32), ((16, VARS), F32), ((HELD, LAT_DEV, D), F32)],
        )(parts, own, lower)
    )


def solution(mesh):
    wide = Mesh(mesh.devices.reshape(4, 8, 4, 2), ("ens", *BAND))
    in_specs = (
        P("ens", BAND, None),
        P("ens", BAND, None),
        P(),
        P(),
        P(),
        P(None, BAND),
        P(None, BAND),
    )
    out_specs = (P(BAND, None), P(BAND, None), P(BAND, None), P("ens", BAND, None))
    return jax.shard_map(
        on_device, mesh=wide, in_specs=in_specs, out_specs=out_specs, check_vma=False
    )
```

```python
import jax
import jax.numpy as jnp
from jax import lax
from jax.experimental import pallas as pl
from jax.experimental.pallas import tpu as pltpu
from jax.sharding import Mesh
from jax.sharding import PartitionSpec as P

HEAD_DIM = 64
CAP = 5.0
DELTA_SQ = 0.0625
EPS = 1e-06

MEMBERS = 8
HELD = 2
GRID_DEV = 128
LAT_DEV = 32
WINDOW = 64
D = 1024
VARS = 100
VARS_PAD = 128
GROUP = 256
GROUPS = D // GROUP
BAND = ("z", "x", "y")
ENS = 4
NEAR = 8
STEPS = ((2, 0), (2, 1), (0, 1), (1, 1), (3, 0), (1, 0), (3, 1))
PATHS = ((1, 0), (3, 0), (0, 1), (1, 1), (3, 0), (1, 0), (3, 1))
FAR = 8
SHARE = 16
COLS = 2 * D // ENS
HELD_ROWS = HELD * LAT_DEV
PRED_ROW = HELD_ROWS * GROUPS

F32 = jnp.float32
LOW = jnp.bfloat16


def slope(offset):
    return offset * lax.rsqrt(offset * offset + DELTA_SQ)


def dot(a, b, a_dim, b_dim):
    return lax.dot_general(a, b, (((a_dim,), (b_dim,)), ((), ())), preferred_element_type=F32)


def same_head():
    rows = lax.broadcasted_iota(jnp.int32, (GROUP, GROUP), 0) // HEAD_DIM
    cols = lax.broadcasted_iota(jnp.int32, (GROUP, GROUP), 1) // HEAD_DIM
    return rows == cols


def by_head(rows, same):
    return jnp.where(same, jnp.concatenate([rows] * 4, axis=0), jnp.zeros((), LOW))


def head_sums(values):
    heads = values.reshape(GROUP // WINDOW, WINDOW, GRID_DEV)
    return heads, jnp.sum(heads, axis=1, keepdims=True)


def shares_of(exp):
    heads, totals = head_sums(exp.astype(F32))
    return (heads * (1.0 / totals)).reshape(GROUP, GRID_DEV)


def from_head(blocks):
    head = lax.broadcasted_iota(jnp.int32, (WINDOW, GROUP), 1) // HEAD_DIM
    total = blocks[:WINDOW]
    for h in range(1, 4):
        total = jnp.where(head == h, blocks[h * WINDOW : (h + 1) * WINDOW], total)
    return total


def own_kernel(latent, edges, key_left, key_right, keys, count):
    rows = jnp.concatenate([latent[0], latent[1]], axis=0)
    keys[:, : D // 2] = dot(rows, key_left[...], 1, 0).astype(LOW)
    keys[:, D // 2 :] = dot(rows, key_right[...], 1, 0).astype(LOW)
    target = edges[0:1, :]
    local = jnp.where(target >= 0, target & (GRID_DEV - 1), -1)
    source = edges[1:2, :] - (target >> 7) * LAT_DEV
    slots = edges.shape[1]
    into = (lax.broadcasted_iota(jnp.int32, (GRID_DEV, slots), 0) == local).astype(F32).astype(LOW)
    node = lax.broadcasted_iota(jnp.int32, (GROUP, slots), 0) & (WINDOW - 1)
    out_of = (node == source).astype(F32).astype(LOW)
    count[...] = dot(out_of, into, 1, 1)


def forward_kernel(
    embed, latent, lat_up, key_left, key_right, value_weight, out_weight, own_keys, edge_count,
    preds, share, normed_low, inverse, exps, damps, values,
    keys, mixed,
):
    rows = jnp.concatenate([latent[0], lat_up[0], latent[1], lat_up[1]], axis=0)
    values[...] = dot(rows, value_weight[...], 1, 0).astype(LOW)
    rows = jnp.concatenate([lat_up[0], lat_up[1]], axis=0)
    for c, weight in enumerate((key_left, key_right)):
        cols = slice(c * (D // 2), (c + 1) * (D // 2))
        upper_rows = dot(rows, weight[...], 1, 0).astype(LOW)
        for m in range(HELD):
            part = slice(m * LAT_DEV, (m + 1) * LAT_DEV)
            keys[m * WINDOW : m * WINDOW + LAT_DEV, cols] = own_keys[part, cols]
            keys[m * WINDOW + LAT_DEV : (m + 1) * WINDOW, cols] = upper_rows[part]
    count = edge_count[...]
    same = same_head()
    rows = lax.broadcasted_iota(jnp.int32, (GRID_DEV, GRID_DEV), 0)
    cols = lax.broadcasted_iota(jnp.int32, (GRID_DEV, GRID_DEV), 1)
    identity = (rows == cols).astype(F32).astype(LOW)
    for m in range(HELD):
        square = jnp.zeros((GRID_DEV, 1), F32)
        for j in range(GROUPS):
            cols = slice(j * GROUP, (j + 1) * GROUP)
            start = j * HELD_ROWS + m * LAT_DEV
            share[start : start + LAT_DEV] = lat_up[m, :, cols]
            query = embed[m, :, cols]
            key = by_head(keys[m * WINDOW : (m + 1) * WINDOW, cols], same)
            value = by_head(values[m * WINDOW : (m + 1) * WINDOW, cols], same)
            bent = jnp.tanh(dot(key, query, 1, 1) * (HEAD_DIM**-0.5 / CAP))
            exp = (count * jnp.exp(CAP * bent)).astype(LOW)
            exps[m, j] = exp
            damps[m, j] = ((1.0 - bent * bent) * HEAD_DIM**-0.5).astype(LOW)
            turned = dot(identity, shares_of(exp).astype(LOW), 1, 1).astype(LOW)
            attended = dot(turned, value, 1, 0)
            sums = query.astype(F32) + attended
            mixed[:, cols] = sums
            square = square + jnp.sum(sums * sums, axis=1, keepdims=True)
        inv = lax.rsqrt(square * (1.0 / D) + EPS)
        low = (mixed[...] * inv).astype(LOW)
        normed_low[m] = low
        inverse[m] = jnp.broadcast_to(inv, (GRID_DEV, 128))
        pred = dot(out_weight[...], low, 1, 1)
        preds[m] = pred
        share[PRED_ROW:, m * GRID_DEV : (m + 1) * GRID_DEV] = pred.astype(LOW)


def backward_kernel(
    me, embed, out_weight, target, preds, every, normed_low, inverse, exps, damps, values,
    halves, next1, next2, next3, out_grad,
    grad, truth,
):
    truth[...] = jnp.zeros((VARS_PAD, GRID_DEV), F32)
    truth[:VARS, :] = target[...]
    same = same_head()
    pred_grads = []
    for m in range(HELD):
        pred = preds[m]
        pair = jnp.zeros((VARS_PAD, GRID_DEV), F32)
        for e in range(MEMBERS // HELD):
            for k in range(HELD):
                pair = pair + slope(pred - every[e, :, k * GRID_DEV : (k + 1) * GRID_DEV].astype(F32))
        for k in range(HELD):
            pair = pair - slope(pred - preds[k].astype(LOW).astype(F32))
            if k != m:
                pair = pair + slope(pred - preds[k])
        base = slope(pred - truth[...]) * (1.0 / MEMBERS)
        pred_grads.append((base - pair * (1.0 / (MEMBERS * (MEMBERS - 1)))).astype(LOW))
    both = jnp.concatenate(pred_grads, axis=1)
    lows = jnp.concatenate([normed_low[0], normed_low[1]], axis=0)
    out_grad[...] = jnp.transpose(dot(both, lows, 1, 0)).astype(LOW)
    for m in range(HELD):
        slant = jnp.zeros((GRID_DEV, 1), F32)
        turned = jnp.transpose(pred_grads[m].astype(F32)).astype(LOW)
        for j in range(GROUPS):
            cols = slice(j * GROUP, (j + 1) * GROUP)
            part = dot(turned, out_weight[:, cols], 1, 0)
            grad[:, cols] = part
            slant = slant + jnp.sum(part * normed_low[m, :, cols].astype(F32), axis=1, keepdims=True)
        slant = slant * (1.0 / D)
        inv = inverse[m][:, :1]
        for j in range(GROUPS):
            cols = slice(j * GROUP, (j + 1) * GROUP)
            mixed_grad = (inv * (grad[:, cols] - normed_low[m, :, cols].astype(F32) * slant)).astype(LOW)
            value = by_head(values[m * WINDOW : (m + 1) * WINDOW, cols], same)
            weight = shares_of(exps[m, j])
            weight_grad = dot(value, mixed_grad, 1, 1)
            inner = head_sums(weight * weight_grad)[1]
            centred = weight_grad.reshape(GROUP // WINDOW, WINDOW, GRID_DEV) - inner
            raw_grad = weight * centred.reshape(GROUP, GRID_DEV) * damps[m, j].astype(F32)
            key_part = from_head(dot(raw_grad.astype(LOW), embed[m, :, cols], 1, 0))
            value_part = from_head(dot(weight.astype(LOW), mixed_grad, 1, 0))
            at = slice(j % 2 * GROUP, (j % 2 + 1) * GROUP)
            for p, part in ((j // 2, key_part), (2 + j // 2, value_part)):
                start = m * LAT_DEV
                halves[p, start : start + LAT_DEV, at] = part[:LAT_DEV].astype(LOW)
                start = start + HELD_ROWS
                halves[p, start : start + LAT_DEV, at] = part[LAT_DEV:].astype(LOW)
    for k, block in ((1, next1), (2, next2), (3, next3)):
        block[: 2 * HELD_ROWS] = halves[(me[0] & (ENS - 1)) ^ k]
    for f in range(FAR // 2):
        start = pl.multiple_of(((me[0] & 1) ^ 1) * (D // 2) + f * NEAR * SHARE, NEAR * SHARE)
        next1[2 * HELD_ROWS :, f * VARS_PAD : (f + 1) * VARS_PAD] = out_grad[
            pl.ds(start, NEAR * SHARE), :
        ]


def latent_kernel(halves, key_weight, value_weight, own, upper):
    key_grad = jnp.concatenate([halves[0], halves[1]], axis=1)
    value_grad = jnp.concatenate([halves[2], halves[3]], axis=1)
    total = dot(key_grad, key_weight[...], 1, 1) + dot(value_grad, value_weight[...], 1, 1)
    own[...] = total[:HELD_ROWS]
    upper[...] = total[HELD_ROWS:].astype(LOW)


def weight_kernel(
    me, halves, last1, last2, last3, nodes, nodes1, nodes2, nodes3, shares, out_grad,
    upper, keep, *refs,
):
    sends, product, pair = refs[: NEAR - 1], refs[-2], refs[-1]
    rows = jnp.concatenate(
        [halves[me[0] & (ENS - 1)], last1[: 2 * HELD_ROWS], last2[...], last3[...]], axis=0
    )
    for j in range(GROUPS):
        cols = slice(j * GROUP, (j + 1) * GROUP)
        at = slice(j * HELD_ROWS, (j + 1) * HELD_ROWS)
        left = []
        for k, block in enumerate((nodes, nodes1, nodes2, nodes3)):
            left += [block[0, :, cols], block[1, :, cols], shares[(me[0] & (ENS - 1)) ^ k, at]]
        left = jnp.concatenate(left, axis=0)
        product[cols, :] = dot(left, rows, 0, 0).astype(LOW)
    for f in range(FAR // 2):
        start = pl.multiple_of((me[0] & 1) * (D // 2) + f * NEAR * SHARE, NEAR * SHARE)
        lanes = slice(f * VARS_PAD, (f + 1) * VARS_PAD)
        own = out_grad[pl.ds(start, NEAR * SHARE), :].astype(F32)
        pair[:, lanes] = (own + last1[2 * HELD_ROWS :, lanes].astype(F32)).astype(LOW)
    for (dx, dy), send in zip(((0, 0), *STEPS), (keep, *sends)):
        near = (((me[0] >> 3) + dx) & 3) * 2 + (((me[0] >> 2) + dy) & 1)
        for far in range(FAR):
            start = pl.multiple_of((far * NEAR + near) * SHARE, SHARE)
            send[far * SHARE : (far + 1) * SHARE] = product[pl.ds(start, SHARE), :]
        start = pl.multiple_of(near * SHARE, SHARE)
        send[FAR * SHARE :] = pair[pl.ds(start, SHARE), :]


def relay_kernel(up, down, held6, held7, send6, send7):
    send6[...] = (held6[...].astype(F32) + up[...].astype(F32)).astype(LOW)
    send7[...] = (held7[...].astype(F32) + down[...].astype(F32)).astype(LOW)


def near_sum_kernel(me, first, *refs):
    value, total = first[...].astype(F32), refs[-1]
    for part in refs[:-1]:
        value = value + part[...].astype(F32)
    for far in range(FAR):
        total[far, :, :COLS] = value[far * SHARE : (far + 1) * SHARE].astype(LOW)
        f = far % (FAR // 2)
        held = jnp.where((me[0] & 1) == far // (FAR // 2), 1.0, 0.0)
        block = value[FAR * SHARE :, f * VARS_PAD : (f + 1) * VARS_PAD]
        total[far, :, COLS:] = (block * held).astype(LOW)


def sum_kernel(parts, total):
    value = parts[0].astype(F32)
    for p in range(1, parts.shape[0]):
        value = value + parts[p].astype(F32)
    total[...] = value.astype(LOW)


def finish_kernel(
    me, mine, part1, part2, part3, own, lower,
    key_weight_grad, value_weight_grad, out_weight_grad, grad_latent,
    parts,
):
    for m in range(HELD):
        rows = slice(m * LAT_DEV, (m + 1) * LAT_DEV)
        grad_latent[m] = own[rows] + lower[rows].astype(F32)
    for k, part in enumerate((mine, part1, part2, part3)):
        parts[(me[0] & (ENS - 1)) ^ k] = part[...]
    total = parts[0, :, COLS:].astype(F32)
    for e in range(1, ENS):
        total = total + parts[e, :, COLS:].astype(F32)
    out_weight_grad[...] = total[:, :VARS]
    for p in range(2):
        key_weight_grad[:, p * COLS : (p + 1) * COLS] = parts[p, :, :COLS].astype(F32)
        value_weight_grad[:, p * COLS : (p + 1) * COLS] = parts[2 + p, :, :COLS].astype(F32)


def whole(shape):
    return pl.BlockSpec(shape, lambda i: (0,) * len(shape))


def call(kernel, outs, scratch=(), specs=None, flops=10**8, bytes_accessed=4 * 10**6):
    def run(*operands):
        places = specs or {}
        return pl.pallas_call(
            kernel,
            grid=(1,),
            in_specs=[places.get(i, whole(value.shape)) for i, value in enumerate(operands)],
            out_specs=[whole(shape) for shape, _ in outs],
            out_shape=[jax.ShapeDtypeStruct(shape, kind) for shape, kind in outs],
            scratch_shapes=[pltpu.VMEM(shape, kind) for shape, kind in scratch],
            compiler_params=pltpu.CompilerParams(vmem_limit_bytes=40 * 2**20),
            cost_estimate=pl.CostEstimate(
                flops=flops, bytes_accessed=bytes_accessed, transcendentals=0
            ),
            name=kernel.__name__,
        )(*operands)

    return run


def band_shift(value, by):
    return lax.ppermute(value, BAND, [(i, i + by) for i in range(64) if 0 <= i + by < 64])


def ens_swap(value, k):
    return lax.ppermute(value, "ens", [(e, e ^ k) for e in range(ENS)])


def near_shift(value, dx, dy):
    pairs = [(x * 2 + y, (x + dx) % 4 * 2 + (y + dy) % 2) for x in range(4) for y in range(2)]
    return lax.ppermute(value, ("x", "y"), pairs)


def on_device(grid_embed, latent, key_weight, value_weight, out_weight, target, edges):
    out_rows = jnp.pad(out_weight, ((0, VARS_PAD - VARS), (0, 0)))
    upper_latent = band_shift(latent, -1)
    nodes1, nodes2 = ens_swap(latent, 1), ens_swap(latent, 2)
    nodes3 = ens_swap(nodes2, 1)
    halves_of_key = (key_weight[:, : D // 2], key_weight[:, D // 2 :])
    own_keys, count = call(own_kernel, [((HELD_ROWS, D), LOW), ((GROUP, GRID_DEV), F32)])(
        latent, edges, *halves_of_key
    )
    preds, share, normed_low, inverse, exps, damps, values = call(
        forward_kernel,
        [
            ((HELD, VARS_PAD, GRID_DEV), F32),
            ((PRED_ROW + VARS_PAD, GROUP), LOW),
            ((HELD, GRID_DEV, D), LOW),
            ((HELD, GRID_DEV, 128), F32),
            ((HELD, GROUPS, GROUP, GRID_DEV), LOW),
            ((HELD, GROUPS, GROUP, GRID_DEV), LOW),
            ((HELD * WINDOW, D), LOW),
        ],
        [((HELD * WINDOW, D), LOW), ((GRID_DEV, D), F32)],
    )(
        grid_embed, latent, upper_latent, *halves_of_key, value_weight, out_rows, own_keys, count
    )
    spot = (lax.axis_index("x") * 2 + lax.axis_index("y")) * ENS + lax.axis_index("ens")
    me = spot.reshape(1)
    shares = lax.all_gather(share, "ens", axis=0)
    block = (2 * HELD_ROWS, COLS)
    scalar = {0: pl.BlockSpec(memory_space=pltpu.SMEM)}
    halves, next1, next2, next3, out_grad = call(
        backward_kernel,
        [((ENS, *block), LOW), ((2 * HELD_ROWS + NEAR * SHARE, COLS), LOW)]
        + [(block, LOW)] * 2
        + [((D, VARS_PAD), LOW)],
        [((GRID_DEV, D), F32), ((VARS_PAD, GRID_DEV), F32)],
        {**scalar, 5: pl.BlockSpec((ENS, VARS_PAD, GROUP), lambda i: (0, PRED_ROW // VARS_PAD, 0))},
    )(me, grid_embed, out_rows, target, preds, shares, normed_low, inverse, exps, damps, values)
    last1, last2, last3 = (ens_swap(v, k) for k, v in ((1, next1), (2, next2), (3, next3)))
    own, upper = call(latent_kernel, [((HELD_ROWS, D), F32), ((HELD_ROWS, D), LOW)])(
        halves, key_weight, value_weight
    )
    lower = band_shift(upper, 1)
    share_block = ((FAR + 1) * SHARE, COLS)
    keep, *sends = call(
        weight_kernel,
        [(share_block, LOW)] * NEAR,
        [((D, COLS), LOW), ((NEAR * SHARE, COLS), LOW)],
        specs={
            **{i: pl.BlockSpec(memory_space=pltpu.SMEM) for i in range(1)},
            9: pl.BlockSpec((ENS, PRED_ROW, GROUP), lambda i: (0, 0, 0)),
            11: pl.BlockSpec((16, 128), lambda i: (0, 0)),
        },
    )(
        me, halves, last1, last2, last3, latent, nodes1, nodes2, nodes3, shares,
        out_grad, upper,
    )
    parts = [near_shift(value, *step) for step, value in zip(PATHS[:5], sends[:5])]
    relayed = call(relay_kernel, [(share_block, LOW), (share_block, LOW)])(
        parts[0], parts[1], sends[5], sends[6]
    )
    parts = parts[2:] + [near_shift(value, *step) for step, value in zip(PATHS[5:], relayed)]
    (total,) = call(near_sum_kernel, [((FAR, SHARE, COLS + VARS_PAD), LOW)], specs=scalar)(
        me, keep, *parts
    )
    parts = lax.all_to_all(total, "z", 0, 0, tiled=True)
    (total,) = call(sum_kernel, [((SHARE, COLS + VARS_PAD), LOW)])(parts)
    parts = [ens_swap(total, k) for k in (1, 2, 3)]
    return tuple(
        call(
            finish_kernel,
            [((16, D), F32), ((16, D), F32), ((16, VARS), F32), ((HELD, LAT_DEV, D), F32)],
            [((ENS, SHARE, COLS + VARS_PAD), LOW)],
            scalar,
        )(me, total, *parts, own, lower)
    )


def solution(mesh):
    wide = Mesh(mesh.devices.reshape(4, 8, 4, 2), ("ens", *BAND))
    in_specs = (
        P("ens", BAND, None),
        P("ens", BAND, None),
        P(),
        P(),
        P(),
        P(None, BAND),
        P(None, BAND),
    )
    out_specs = (P(BAND, None), P(BAND, None), P(BAND, None), P("ens", BAND, None))
    return jax.shard_map(
        on_device, mesh=wide, in_specs=in_specs, out_specs=out_specs, check_vma=False
    )
```

```python
import jax
import jax.numpy as jnp
from jax import lax
from jax.experimental import pallas as pl
from jax.experimental.pallas import tpu as pltpu
from jax.sharding import Mesh
from jax.sharding import PartitionSpec as P

HEAD_DIM = 64
CAP = 5.0
DELTA_SQ = 0.0625
EPS = 1e-06

MEMBERS = 8
HELD = 2
GRID_DEV = 128
LAT_DEV = 32
WINDOW = 64
D = 1024
VARS = 100
VARS_PAD = 128
GROUP = 256
GROUPS = D // GROUP
BAND = ("z", "x", "y")
ENS = 4
NEAR = 8
STEPS = ((2, 0), (2, 1), (1, 1), (3, 0), (1, 0), (3, 1), (0, 1))
PATHS = ((1, 0), (3, 0), (1, 0), (3, 0), (1, 0), (3, 1), (0, 1))
FAR = 8
SHARE = 16
COLS = 2 * D // ENS
HELD_ROWS = HELD * LAT_DEV
PRED_ROW = HELD_ROWS * GROUPS

F32 = jnp.float32
LOW = jnp.bfloat16


def slope(offset):
    return offset * lax.rsqrt(offset * offset + DELTA_SQ)


def dot(a, b, a_dim, b_dim):
    return lax.dot_general(a, b, (((a_dim,), (b_dim,)), ((), ())), preferred_element_type=F32)


def same_head():
    rows = lax.broadcasted_iota(jnp.int32, (GROUP, GROUP), 0) // HEAD_DIM
    cols = lax.broadcasted_iota(jnp.int32, (GROUP, GROUP), 1) // HEAD_DIM
    return rows == cols


def by_head(rows, same):
    return jnp.where(same, jnp.concatenate([rows] * 4, axis=0), jnp.zeros((), LOW))


def head_sums(values):
    heads = values.reshape(GROUP // WINDOW, WINDOW, GRID_DEV)
    return heads, jnp.sum(heads, axis=1, keepdims=True)


def shares_of(exp):
    heads, totals = head_sums(exp.astype(F32))
    return (heads * (1.0 / totals)).reshape(GROUP, GRID_DEV)


def from_head(blocks):
    head = lax.broadcasted_iota(jnp.int32, (WINDOW, GROUP), 1) // HEAD_DIM
    total = blocks[:WINDOW]
    for h in range(1, 4):
        total = jnp.where(head == h, blocks[h * WINDOW : (h + 1) * WINDOW], total)
    return total


def own_kernel(latent, edges, key_left, key_right, keys, count):
    rows = jnp.concatenate([latent[0], latent[1]], axis=0)
    keys[:, : D // 2] = dot(rows, key_left[...], 1, 0).astype(LOW)
    keys[:, D // 2 :] = dot(rows, key_right[...], 1, 0).astype(LOW)
    target = edges[0:1, :]
    local = jnp.where(target >= 0, target & (GRID_DEV - 1), -1)
    source = edges[1:2, :] - (target >> 7) * LAT_DEV
    slots = edges.shape[1]
    into = (lax.broadcasted_iota(jnp.int32, (GRID_DEV, slots), 0) == local).astype(F32).astype(LOW)
    node = lax.broadcasted_iota(jnp.int32, (GROUP, slots), 0) & (WINDOW - 1)
    out_of = (node == source).astype(F32).astype(LOW)
    count[...] = dot(out_of, into, 1, 1)


def forward_kernel(
    embed, latent, lat_up, key_left, key_right, value_weight, out_weight, own_keys, edge_count,
    preds, share, normed_low, inverse, exps, damps, values,
    keys, mixed,
):
    rows = jnp.concatenate([latent[0], lat_up[0], latent[1], lat_up[1]], axis=0)
    values[...] = dot(rows, value_weight[...], 1, 0).astype(LOW)
    rows = jnp.concatenate([lat_up[0], lat_up[1]], axis=0)
    for c, weight in enumerate((key_left, key_right)):
        cols = slice(c * (D // 2), (c + 1) * (D // 2))
        upper_rows = dot(rows, weight[...], 1, 0).astype(LOW)
        for m in range(HELD):
            part = slice(m * LAT_DEV, (m + 1) * LAT_DEV)
            keys[m * WINDOW : m * WINDOW + LAT_DEV, cols] = own_keys[part, cols]
            keys[m * WINDOW + LAT_DEV : (m + 1) * WINDOW, cols] = upper_rows[part]
    count = edge_count[...]
    same = same_head()
    rows = lax.broadcasted_iota(jnp.int32, (GRID_DEV, GRID_DEV), 0)
    cols = lax.broadcasted_iota(jnp.int32, (GRID_DEV, GRID_DEV), 1)
    identity = (rows == cols).astype(F32).astype(LOW)
    for m in range(HELD):
        square = jnp.zeros((GRID_DEV, 1), F32)
        for j in range(GROUPS):
            cols = slice(j * GROUP, (j + 1) * GROUP)
            start = j * HELD_ROWS + m * LAT_DEV
            share[start : start + LAT_DEV] = lat_up[m, :, cols]
            query = embed[m, :, cols]
            key = by_head(keys[m * WINDOW : (m + 1) * WINDOW, cols], same)
            value = by_head(values[m * WINDOW : (m + 1) * WINDOW, cols], same)
            bent = jnp.tanh(dot(key, query, 1, 1) * (HEAD_DIM**-0.5 / CAP))
            exp = (count * jnp.exp(CAP * bent)).astype(LOW)
            exps[m, j] = exp
            damps[m, j] = ((1.0 - bent * bent) * HEAD_DIM**-0.5).astype(LOW)
            turned = dot(identity, shares_of(exp).astype(LOW), 1, 1).astype(LOW)
            attended = dot(turned, value, 1, 0)
            sums = query.astype(F32) + attended
            mixed[:, cols] = sums
            square = square + jnp.sum(sums * sums, axis=1, keepdims=True)
        inv = lax.rsqrt(square * (1.0 / D) + EPS)
        low = (mixed[...] * inv).astype(LOW)
        normed_low[m] = low
        inverse[m] = jnp.broadcast_to(inv, (GRID_DEV, 128))
        pred = dot(out_weight[...], low, 1, 1)
        preds[m] = pred
        share[PRED_ROW:, m * GRID_DEV : (m + 1) * GRID_DEV] = pred.astype(LOW)


def backward_kernel(
    me, embed, out_weight, target, preds, every, normed_low, inverse, exps, damps, values,
    halves, next1, next2, next3, out_grad,
    grad, truth,
):
    truth[...] = jnp.zeros((VARS_PAD, GRID_DEV), F32)
    truth[:VARS, :] = target[...]
    same = same_head()
    pred_grads = []
    for m in range(HELD):
        pred = preds[m]
        pair = jnp.zeros((VARS_PAD, GRID_DEV), F32)
        for e in range(MEMBERS // HELD):
            for k in range(HELD):
                pair = pair + slope(pred - every[e, :, k * GRID_DEV : (k + 1) * GRID_DEV].astype(F32))
        for k in range(HELD):
            pair = pair - slope(pred - preds[k].astype(LOW).astype(F32))
            if k != m:
                pair = pair + slope(pred - preds[k])
        base = slope(pred - truth[...]) * (1.0 / MEMBERS)
        pred_grads.append((base - pair * (1.0 / (MEMBERS * (MEMBERS - 1)))).astype(LOW))
    both = jnp.concatenate(pred_grads, axis=1)
    lows = jnp.concatenate([normed_low[0], normed_low[1]], axis=0)
    out_grad[...] = jnp.transpose(dot(both, lows, 1, 0)).astype(LOW)
    for m in range(HELD):
        slant = jnp.zeros((GRID_DEV, 1), F32)
        turned = jnp.transpose(pred_grads[m].astype(F32)).astype(LOW)
        for j in range(GROUPS):
            cols = slice(j * GROUP, (j + 1) * GROUP)
            part = dot(turned, out_weight[:, cols], 1, 0)
            grad[:, cols] = part
            slant = slant + jnp.sum(part * normed_low[m, :, cols].astype(F32), axis=1, keepdims=True)
        slant = slant * (1.0 / D)
        inv = inverse[m][:, :1]
        for j in range(GROUPS):
            cols = slice(j * GROUP, (j + 1) * GROUP)
            mixed_grad = (inv * (grad[:, cols] - normed_low[m, :, cols].astype(F32) * slant)).astype(LOW)
            value = by_head(values[m * WINDOW : (m + 1) * WINDOW, cols], same)
            weight = shares_of(exps[m, j])
            weight_grad = dot(value, mixed_grad, 1, 1)
            inner = head_sums(weight * weight_grad)[1]
            centred = weight_grad.reshape(GROUP // WINDOW, WINDOW, GRID_DEV) - inner
            raw_grad = weight * centred.reshape(GROUP, GRID_DEV) * damps[m, j].astype(F32)
            key_part = from_head(dot(raw_grad.astype(LOW), embed[m, :, cols], 1, 0))
            value_part = from_head(dot(weight.astype(LOW), mixed_grad, 1, 0))
            at = slice(j % 2 * GROUP, (j % 2 + 1) * GROUP)
            for p, part in ((j // 2, key_part), (2 + j // 2, value_part)):
                start = m * LAT_DEV
                halves[p, start : start + LAT_DEV, at] = part[:LAT_DEV].astype(LOW)
                start = start + HELD_ROWS
                halves[p, start : start + LAT_DEV, at] = part[LAT_DEV:].astype(LOW)
    for k, block in ((1, next1), (2, next2), (3, next3)):
        block[: 2 * HELD_ROWS] = halves[(me[0] & (ENS - 1)) ^ k]
    for f in range(FAR // 2):
        start = pl.multiple_of(((me[0] & 1) ^ 1) * (D // 2) + f * NEAR * SHARE, NEAR * SHARE)
        next1[2 * HELD_ROWS :, f * VARS_PAD : (f + 1) * VARS_PAD] = out_grad[
            pl.ds(start, NEAR * SHARE), :
        ]


def latent_kernel(halves, key_weight, value_weight, own, upper):
    key_grad = jnp.concatenate([halves[0], halves[1]], axis=1)
    value_grad = jnp.concatenate([halves[2], halves[3]], axis=1)
    total = dot(key_grad, key_weight[...], 1, 1) + dot(value_grad, value_weight[...], 1, 1)
    own[...] = total[:HELD_ROWS]
    upper[...] = total[HELD_ROWS:].astype(LOW)


def weight_kernel(
    me, halves, last1, last2, last3, nodes, nodes1, nodes2, nodes3, shares, out_grad,
    upper, keep, *refs,
):
    sends, product, pair = refs[: NEAR - 1], refs[-2], refs[-1]
    rows = jnp.concatenate(
        [halves[me[0] & (ENS - 1)], last1[: 2 * HELD_ROWS], last2[...], last3[...]], axis=0
    )
    for j in range(GROUPS):
        cols = slice(j * GROUP, (j + 1) * GROUP)
        at = slice(j * HELD_ROWS, (j + 1) * HELD_ROWS)
        left = []
        for k, block in enumerate((nodes, nodes1, nodes2, nodes3)):
            left += [block[0, :, cols], block[1, :, cols], shares[(me[0] & (ENS - 1)) ^ k, at]]
        left = jnp.concatenate(left, axis=0)
        product[cols, :] = dot(left, rows, 0, 0).astype(LOW)
    for f in range(FAR // 2):
        start = pl.multiple_of((me[0] & 1) * (D // 2) + f * NEAR * SHARE, NEAR * SHARE)
        lanes = slice(f * VARS_PAD, (f + 1) * VARS_PAD)
        own = out_grad[pl.ds(start, NEAR * SHARE), :].astype(F32)
        pair[:, lanes] = (own + last1[2 * HELD_ROWS :, lanes].astype(F32)).astype(LOW)
    for (dx, dy), send in zip(((0, 0), *STEPS), (keep, *sends)):
        near = (((me[0] >> 3) + dx) & 3) * 2 + (((me[0] >> 2) + dy) & 1)
        for far in range(FAR):
            start = pl.multiple_of((far * NEAR + near) * SHARE, SHARE)
            send[far * SHARE : (far + 1) * SHARE] = product[pl.ds(start, SHARE), :]
        start = pl.multiple_of(near * SHARE, SHARE)
        send[FAR * SHARE :] = pair[pl.ds(start, SHARE), :]


def relay_kernel(up, down, side, held5, held6, held7, send5, send6, send7):
    for part, held, send in ((up, held5, send5), (down, held6, send6), (side, held7, send7)):
        send[...] = (held[...].astype(F32) + part[...].astype(F32)).astype(LOW)


def near_sum_kernel(me, first, *refs):
    value, total = first[...].astype(F32), refs[-1]
    for part in refs[:-1]:
        value = value + part[...].astype(F32)
    for far in range(FAR):
        total[far, :, :COLS] = value[far * SHARE : (far + 1) * SHARE].astype(LOW)
        f = far % (FAR // 2)
        held = jnp.where((me[0] & 1) == far // (FAR // 2), 1.0, 0.0)
        block = value[FAR * SHARE :, f * VARS_PAD : (f + 1) * VARS_PAD]
        total[far, :, COLS:] = (block * held).astype(LOW)


def sum_kernel(parts, total):
    value = parts[0].astype(F32)
    for p in range(1, parts.shape[0]):
        value = value + parts[p].astype(F32)
    total[...] = value.astype(LOW)


def finish_kernel(
    me, mine, part1, part2, part3, own, lower,
    key_weight_grad, value_weight_grad, out_weight_grad, grad_latent,
    parts,
):
    for m in range(HELD):
        rows = slice(m * LAT_DEV, (m + 1) * LAT_DEV)
        grad_latent[m] = own[rows] + lower[rows].astype(F32)
    for k, part in enumerate((mine, part1, part2, part3)):
        parts[(me[0] & (ENS - 1)) ^ k] = part[...]
    total = parts[0, :, COLS:].astype(F32)
    for e in range(1, ENS):
        total = total + parts[e, :, COLS:].astype(F32)
    out_weight_grad[...] = total[:, :VARS]
    for p in range(2):
        key_weight_grad[:, p * COLS : (p + 1) * COLS] = parts[p, :, :COLS].astype(F32)
        value_weight_grad[:, p * COLS : (p + 1) * COLS] = parts[2 + p, :, :COLS].astype(F32)


def whole(shape):
    return pl.BlockSpec(shape, lambda i: (0,) * len(shape))


def call(kernel, outs, scratch=(), specs=None, flops=10**8, bytes_accessed=4 * 10**6):
    def run(*operands):
        places = specs or {}
        return pl.pallas_call(
            kernel,
            grid=(1,),
            in_specs=[places.get(i, whole(value.shape)) for i, value in enumerate(operands)],
            out_specs=[whole(shape) for shape, _ in outs],
            out_shape=[jax.ShapeDtypeStruct(shape, kind) for shape, kind in outs],
            scratch_shapes=[pltpu.VMEM(shape, kind) for shape, kind in scratch],
            compiler_params=pltpu.CompilerParams(vmem_limit_bytes=40 * 2**20),
            cost_estimate=pl.CostEstimate(
                flops=flops, bytes_accessed=bytes_accessed, transcendentals=0
            ),
            name=kernel.__name__,
        )(*operands)

    return run


def band_shift(value, by):
    return lax.ppermute(value, BAND, [(i, i + by) for i in range(64) if 0 <= i + by < 64])


def ens_swap(value, k):
    return lax.ppermute(value, "ens", [(e, e ^ k) for e in range(ENS)])


def near_shift(value, dx, dy):
    pairs = [(x * 2 + y, (x + dx) % 4 * 2 + (y + dy) % 2) for x in range(4) for y in range(2)]
    return lax.ppermute(value, ("x", "y"), pairs)


def on_device(grid_embed, latent, key_weight, value_weight, out_weight, target, edges):
    out_rows = jnp.pad(out_weight, ((0, VARS_PAD - VARS), (0, 0)))
    upper_latent = band_shift(latent, -1)
    nodes1, nodes2 = ens_swap(latent, 1), ens_swap(latent, 2)
    nodes3 = ens_swap(nodes2, 1)
    halves_of_key = (key_weight[:, : D // 2], key_weight[:, D // 2 :])
    own_keys, count = call(own_kernel, [((HELD_ROWS, D), LOW), ((GROUP, GRID_DEV), F32)])(
        latent, edges, *halves_of_key
    )
    preds, share, normed_low, inverse, exps, damps, values = call(
        forward_kernel,
        [
            ((HELD, VARS_PAD, GRID_DEV), F32),
            ((PRED_ROW + VARS_PAD, GROUP), LOW),
            ((HELD, GRID_DEV, D), LOW),
            ((HELD, GRID_DEV, 128), F32),
            ((HELD, GROUPS, GROUP, GRID_DEV), LOW),
            ((HELD, GROUPS, GROUP, GRID_DEV), LOW),
            ((HELD * WINDOW, D), LOW),
        ],
        [((HELD * WINDOW, D), LOW), ((GRID_DEV, D), F32)],
    )(
        grid_embed, latent, upper_latent, *halves_of_key, value_weight, out_rows, own_keys, count
    )
    spot = (lax.axis_index("x") * 2 + lax.axis_index("y")) * ENS + lax.axis_index("ens")
    me = spot.reshape(1)
    shares = lax.all_gather(share, "ens", axis=0)
    block = (2 * HELD_ROWS, COLS)
    scalar = {0: pl.BlockSpec(memory_space=pltpu.SMEM)}
    halves, next1, next2, next3, out_grad = call(
        backward_kernel,
        [((ENS, *block), LOW), ((2 * HELD_ROWS + NEAR * SHARE, COLS), LOW)]
        + [(block, LOW)] * 2
        + [((D, VARS_PAD), LOW)],
        [((GRID_DEV, D), F32), ((VARS_PAD, GRID_DEV), F32)],
        {**scalar, 5: pl.BlockSpec((ENS, VARS_PAD, GROUP), lambda i: (0, PRED_ROW // VARS_PAD, 0))},
    )(me, grid_embed, out_rows, target, preds, shares, normed_low, inverse, exps, damps, values)
    last1, last2, last3 = (ens_swap(v, k) for k, v in ((1, next1), (2, next2), (3, next3)))
    own, upper = call(latent_kernel, [((HELD_ROWS, D), F32), ((HELD_ROWS, D), LOW)])(
        halves, key_weight, value_weight
    )
    lower = band_shift(upper, 1)
    share_block = ((FAR + 1) * SHARE, COLS)
    keep, *sends = call(
        weight_kernel,
        [(share_block, LOW)] * NEAR,
        [((D, COLS), LOW), ((NEAR * SHARE, COLS), LOW)],
        specs={
            **{i: pl.BlockSpec(memory_space=pltpu.SMEM) for i in range(1)},
            9: pl.BlockSpec((ENS, PRED_ROW, GROUP), lambda i: (0, 0, 0)),
            11: pl.BlockSpec((16, 128), lambda i: (0, 0)),
        },
    )(
        me, halves, last1, last2, last3, latent, nodes1, nodes2, nodes3, shares,
        out_grad, upper,
    )
    parts = [near_shift(value, *step) for step, value in zip(PATHS[:4], sends[:4])]
    relayed = call(relay_kernel, [(share_block, LOW)] * 3)(*parts[:3], *sends[4:])
    parts = parts[3:] + [near_shift(value, *step) for step, value in zip(PATHS[4:], relayed)]
    (total,) = call(near_sum_kernel, [((FAR, SHARE, COLS + VARS_PAD), LOW)], specs=scalar)(
        me, keep, *parts
    )
    parts = lax.all_to_all(total, "z", 0, 0, tiled=True)
    (total,) = call(sum_kernel, [((SHARE, COLS + VARS_PAD), LOW)])(parts)
    parts = [ens_swap(total, k) for k in (1, 2, 3)]
    return tuple(
        call(
            finish_kernel,
            [((16, D), F32), ((16, D), F32), ((16, VARS), F32), ((HELD, LAT_DEV, D), F32)],
            [((ENS, SHARE, COLS + VARS_PAD), LOW)],
            scalar,
        )(me, total, *parts, own, lower)
    )


def solution(mesh):
    wide = Mesh(mesh.devices.reshape(4, 8, 4, 2), ("ens", *BAND))
    in_specs = (
        P("ens", BAND, None),
        P("ens", BAND, None),
        P(),
        P(),
        P(),
        P(None, BAND),
        P(None, BAND),
    )
    out_specs = (P(BAND, None), P(BAND, None), P(BAND, None), P("ens", BAND, None))
    return jax.shard_map(
        on_device, mesh=wide, in_specs=in_specs, out_specs=out_specs, check_vma=False
    )
```

```python
import jax
import jax.numpy as jnp
from jax import lax
from jax.experimental import pallas as pl
from jax.experimental.pallas import tpu as pltpu
from jax.sharding import Mesh
from jax.sharding import PartitionSpec as P

HEAD_DIM = 64
CAP = 5.0
DELTA_SQ = 0.0625
EPS = 1e-06

MEMBERS = 8
HELD = 2
GRID_DEV = 128
LAT_DEV = 32
WINDOW = 64
D = 1024
VARS = 100
VARS_PAD = 128
GROUP = 256
GROUPS = D // GROUP
BAND = ("z", "x", "y")
ENS = 4
NEAR = 8
STEPS = ((2, 0), (2, 1), (0, 1), (1, 1), (3, 0), (3, 1), (1, 0))
PATHS = ((1, 0), (3, 0), (0, 1), (1, 1), (3, 0), (3, 1), (1, 0))
FAR = 8
SHARE = 16
COLS = 2 * D // ENS
HELD_ROWS = HELD * LAT_DEV
PRED_ROW = HELD_ROWS * GROUPS

F32 = jnp.float32
LOW = jnp.bfloat16


def slope(offset):
    return offset * lax.rsqrt(offset * offset + DELTA_SQ)


def dot(a, b, a_dim, b_dim):
    return lax.dot_general(a, b, (((a_dim,), (b_dim,)), ((), ())), preferred_element_type=F32)


def same_head():
    rows = lax.broadcasted_iota(jnp.int32, (GROUP, GROUP), 0) // HEAD_DIM
    cols = lax.broadcasted_iota(jnp.int32, (GROUP, GROUP), 1) // HEAD_DIM
    return rows == cols


def by_head(rows, same):
    return jnp.where(same, jnp.concatenate([rows] * 4, axis=0), jnp.zeros((), LOW))


def head_sums(values):
    heads = values.reshape(GROUP // WINDOW, WINDOW, GRID_DEV)
    return heads, jnp.sum(heads, axis=1, keepdims=True)


def shares_of(exp):
    heads, totals = head_sums(exp.astype(F32))
    return (heads * (1.0 / totals)).reshape(GROUP, GRID_DEV)


def from_head(blocks):
    head = lax.broadcasted_iota(jnp.int32, (WINDOW, GROUP), 1) // HEAD_DIM
    total = blocks[:WINDOW]
    for h in range(1, 4):
        total = jnp.where(head == h, blocks[h * WINDOW : (h + 1) * WINDOW], total)
    return total


def own_kernel(latent, edges, key_left, key_right, keys, count):
    rows = jnp.concatenate([latent[0], latent[1]], axis=0)
    keys[:, : D // 2] = dot(rows, key_left[...], 1, 0).astype(LOW)
    keys[:, D // 2 :] = dot(rows, key_right[...], 1, 0).astype(LOW)
    target = edges[0:1, :]
    local = jnp.where(target >= 0, target & (GRID_DEV - 1), -1)
    source = edges[1:2, :] - (target >> 7) * LAT_DEV
    slots = edges.shape[1]
    into = (lax.broadcasted_iota(jnp.int32, (GRID_DEV, slots), 0) == local).astype(F32).astype(LOW)
    node = lax.broadcasted_iota(jnp.int32, (GROUP, slots), 0) & (WINDOW - 1)
    out_of = (node == source).astype(F32).astype(LOW)
    count[...] = dot(out_of, into, 1, 1)


def forward_kernel(
    embed, latent, lat_up, key_left, key_right, value_weight, out_weight, own_keys, edge_count,
    preds, share, normed_low, inverse, exps, damps, values,
    keys, mixed,
):
    rows = jnp.concatenate([latent[0], lat_up[0], latent[1], lat_up[1]], axis=0)
    values[...] = dot(rows, value_weight[...], 1, 0).astype(LOW)
    rows = jnp.concatenate([lat_up[0], lat_up[1]], axis=0)
    for c, weight in enumerate((key_left, key_right)):
        cols = slice(c * (D // 2), (c + 1) * (D // 2))
        upper_rows = dot(rows, weight[...], 1, 0).astype(LOW)
        for m in range(HELD):
            part = slice(m * LAT_DEV, (m + 1) * LAT_DEV)
            keys[m * WINDOW : m * WINDOW + LAT_DEV, cols] = own_keys[part, cols]
            keys[m * WINDOW + LAT_DEV : (m + 1) * WINDOW, cols] = upper_rows[part]
    count = edge_count[...]
    same = same_head()
    rows = lax.broadcasted_iota(jnp.int32, (GRID_DEV, GRID_DEV), 0)
    cols = lax.broadcasted_iota(jnp.int32, (GRID_DEV, GRID_DEV), 1)
    identity = (rows == cols).astype(F32).astype(LOW)
    for m in range(HELD):
        square = jnp.zeros((GRID_DEV, 1), F32)
        for j in range(GROUPS):
            cols = slice(j * GROUP, (j + 1) * GROUP)
            start = j * HELD_ROWS + m * LAT_DEV
            share[start : start + LAT_DEV] = lat_up[m, :, cols]
            query = embed[m, :, cols]
            key = by_head(keys[m * WINDOW : (m + 1) * WINDOW, cols], same)
            value = by_head(values[m * WINDOW : (m + 1) * WINDOW, cols], same)
            bent = jnp.tanh(dot(key, query, 1, 1) * (HEAD_DIM**-0.5 / CAP))
            exp = (count * jnp.exp(CAP * bent)).astype(LOW)
            exps[m, j] = exp
            damps[m, j] = ((1.0 - bent * bent) * HEAD_DIM**-0.5).astype(LOW)
            turned = dot(identity, shares_of(exp).astype(LOW), 1, 1).astype(LOW)
            attended = dot(turned, value, 1, 0)
            sums = query.astype(F32) + attended
            mixed[:, cols] = sums
            square = square + jnp.sum(sums * sums, axis=1, keepdims=True)
        inv = lax.rsqrt(square * (1.0 / D) + EPS)
        low = (mixed[...] * inv).astype(LOW)
        normed_low[m] = low
        inverse[m] = jnp.broadcast_to(inv, (GRID_DEV, 128))
        pred = dot(out_weight[...], low, 1, 1)
        preds[m] = pred
        share[PRED_ROW:, m * GRID_DEV : (m + 1) * GRID_DEV] = pred.astype(LOW)


def backward_kernel(
    me, embed, out_weight, target, preds, every, normed_low, inverse, exps, damps, values,
    halves, next1, next2, next3, out_grad,
    grad, truth,
):
    truth[...] = jnp.zeros((VARS_PAD, GRID_DEV), F32)
    truth[:VARS, :] = target[...]
    same = same_head()
    pred_grads = []
    for m in range(HELD):
        pred = preds[m]
        pair = jnp.zeros((VARS_PAD, GRID_DEV), F32)
        for e in range(MEMBERS // HELD):
            for k in range(HELD):
                pair = pair + slope(pred - every[e, :, k * GRID_DEV : (k + 1) * GRID_DEV].astype(F32))
        for k in range(HELD):
            pair = pair - slope(pred - preds[k].astype(LOW).astype(F32))
            if k != m:
                pair = pair + slope(pred - preds[k])
        base = slope(pred - truth[...]) * (1.0 / MEMBERS)
        pred_grads.append((base - pair * (1.0 / (MEMBERS * (MEMBERS - 1)))).astype(LOW))
    both = jnp.concatenate(pred_grads, axis=1)
    lows = jnp.concatenate([normed_low[0], normed_low[1]], axis=0)
    out_grad[...] = jnp.transpose(dot(both, lows, 1, 0)).astype(LOW)
    for m in range(HELD):
        slant = jnp.zeros((GRID_DEV, 1), F32)
        turned = jnp.transpose(pred_grads[m].astype(F32)).astype(LOW)
        for j in range(GROUPS):
            cols = slice(j * GROUP, (j + 1) * GROUP)
            part = dot(turned, out_weight[:, cols], 1, 0)
            grad[:, cols] = part
            slant = slant + jnp.sum(part * normed_low[m, :, cols].astype(F32), axis=1, keepdims=True)
        slant = slant * (1.0 / D)
        inv = inverse[m][:, :1]
        for j in range(GROUPS):
            cols = slice(j * GROUP, (j + 1) * GROUP)
            mixed_grad = (inv * (grad[:, cols] - normed_low[m, :, cols].astype(F32) * slant)).astype(LOW)
            value = by_head(values[m * WINDOW : (m + 1) * WINDOW, cols], same)
            weight = shares_of(exps[m, j])
            weight_grad = dot(value, mixed_grad, 1, 1)
            inner = head_sums(weight * weight_grad)[1]
            centred = weight_grad.reshape(GROUP // WINDOW, WINDOW, GRID_DEV) - inner
            raw_grad = weight * centred.reshape(GROUP, GRID_DEV) * damps[m, j].astype(F32)
            key_part = from_head(dot(raw_grad.astype(LOW), embed[m, :, cols], 1, 0))
            value_part = from_head(dot(weight.astype(LOW), mixed_grad, 1, 0))
            at = slice(j % 2 * GROUP, (j % 2 + 1) * GROUP)
            for p, part in ((j // 2, key_part), (2 + j // 2, value_part)):
                start = m * LAT_DEV
                halves[p, start : start + LAT_DEV, at] = part[:LAT_DEV].astype(LOW)
                start = start + HELD_ROWS
                halves[p, start : start + LAT_DEV, at] = part[LAT_DEV:].astype(LOW)
    for k, block in ((1, next1), (2, next2), (3, next3)):
        block[: 2 * HELD_ROWS] = halves[(me[0] & (ENS - 1)) ^ k]
    for f in range(FAR // 2):
        start = pl.multiple_of(((me[0] & 1) ^ 1) * (D // 2) + f * NEAR * SHARE, NEAR * SHARE)
        next1[2 * HELD_ROWS :, f * VARS_PAD : (f + 1) * VARS_PAD] = out_grad[
            pl.ds(start, NEAR * SHARE), :
        ]


def latent_kernel(halves, key_weight, value_weight, own, upper):
    key_grad = jnp.concatenate([halves[0], halves[1]], axis=1)
    value_grad = jnp.concatenate([halves[2], halves[3]], axis=1)
    total = dot(key_grad, key_weight[...], 1, 1) + dot(value_grad, value_weight[...], 1, 1)
    own[...] = total[:HELD_ROWS]
    upper[...] = total[HELD_ROWS:].astype(LOW)


def weight_kernel(
    me, halves, last1, last2, last3, nodes, nodes1, nodes2, nodes3, shares, out_grad,
    upper, keep, *refs,
):
    sends, product, pair = refs[: NEAR - 1], refs[-2], refs[-1]
    rows = jnp.concatenate(
        [halves[me[0] & (ENS - 1)], last1[: 2 * HELD_ROWS], last2[...], last3[...]], axis=0
    )
    for j in range(GROUPS):
        cols = slice(j * GROUP, (j + 1) * GROUP)
        at = slice(j * HELD_ROWS, (j + 1) * HELD_ROWS)
        left = []
        for k, block in enumerate((nodes, nodes1, nodes2, nodes3)):
            left += [block[0, :, cols], block[1, :, cols], shares[(me[0] & (ENS - 1)) ^ k, at]]
        left = jnp.concatenate(left, axis=0)
        product[cols, :] = dot(left, rows, 0, 0).astype(LOW)
    for f in range(FAR // 2):
        start = pl.multiple_of((me[0] & 1) * (D // 2) + f * NEAR * SHARE, NEAR * SHARE)
        lanes = slice(f * VARS_PAD, (f + 1) * VARS_PAD)
        own = out_grad[pl.ds(start, NEAR * SHARE), :].astype(F32)
        pair[:, lanes] = (own + last1[2 * HELD_ROWS :, lanes].astype(F32)).astype(LOW)
    for (dx, dy), send in zip(((0, 0), *STEPS), (keep, *sends)):
        near = (((me[0] >> 3) + dx) & 3) * 2 + (((me[0] >> 2) + dy) & 1)
        for far in range(FAR):
            start = pl.multiple_of((far * NEAR + near) * SHARE, SHARE)
            send[far * SHARE : (far + 1) * SHARE] = product[pl.ds(start, SHARE), :]
        start = pl.multiple_of(near * SHARE, SHARE)
        send[FAR * SHARE :] = pair[pl.ds(start, SHARE), :]


def relay_kernel(up, down, held6, held7, send6, send7):
    send6[...] = (held6[...].astype(F32) + up[...].astype(F32)).astype(LOW)
    send7[...] = (held7[...].astype(F32) + down[...].astype(F32)).astype(LOW)


def near_sum_kernel(me, first, *refs):
    value, total = first[...].astype(F32), refs[-1]
    for part in refs[:-1]:
        value = value + part[...].astype(F32)
    for far in range(FAR):
        total[far, :, :COLS] = value[far * SHARE : (far + 1) * SHARE].astype(LOW)
        f = far % (FAR // 2)
        held = jnp.where((me[0] & 1) == far // (FAR // 2), 1.0, 0.0)
        block = value[FAR * SHARE :, f * VARS_PAD : (f + 1) * VARS_PAD]
        total[far, :, COLS:] = (block * held).astype(LOW)


def sum_kernel(parts, total):
    value = parts[0].astype(F32)
    for p in range(1, parts.shape[0]):
        value = value + parts[p].astype(F32)
    total[...] = value.astype(LOW)


def finish_kernel(
    me, mine, part1, part2, part3, own, lower,
    key_weight_grad, value_weight_grad, out_weight_grad, grad_latent,
    parts,
):
    for m in range(HELD):
        rows = slice(m * LAT_DEV, (m + 1) * LAT_DEV)
        grad_latent[m] = own[rows] + lower[rows].astype(F32)
    for k, part in enumerate((mine, part1, part2, part3)):
        parts[(me[0] & (ENS - 1)) ^ k] = part[...]
    total = parts[0, :, COLS:].astype(F32)
    for e in range(1, ENS):
        total = total + parts[e, :, COLS:].astype(F32)
    out_weight_grad[...] = total[:, :VARS]
    for p in range(2):
        key_weight_grad[:, p * COLS : (p + 1) * COLS] = parts[p, :, :COLS].astype(F32)
        value_weight_grad[:, p * COLS : (p + 1) * COLS] = parts[2 + p, :, :COLS].astype(F32)


def whole(shape):
    return pl.BlockSpec(shape, lambda i: (0,) * len(shape))


def call(kernel, outs, scratch=(), specs=None, flops=10**8, bytes_accessed=4 * 10**6):
    def run(*operands):
        places = specs or {}
        return pl.pallas_call(
            kernel,
            grid=(1,),
            in_specs=[places.get(i, whole(value.shape)) for i, value in enumerate(operands)],
            out_specs=[whole(shape) for shape, _ in outs],
            out_shape=[jax.ShapeDtypeStruct(shape, kind) for shape, kind in outs],
            scratch_shapes=[pltpu.VMEM(shape, kind) for shape, kind in scratch],
            compiler_params=pltpu.CompilerParams(vmem_limit_bytes=40 * 2**20),
            cost_estimate=pl.CostEstimate(
                flops=flops, bytes_accessed=bytes_accessed, transcendentals=0
            ),
            name=kernel.__name__,
        )(*operands)

    return run


def band_shift(value, by):
    return lax.ppermute(value, BAND, [(i, i + by) for i in range(64) if 0 <= i + by < 64])


def ens_swap(value, k):
    return lax.ppermute(value, "ens", [(e, e ^ k) for e in range(ENS)])


def near_shift(value, dx, dy):
    pairs = [(x * 2 + y, (x + dx) % 4 * 2 + (y + dy) % 2) for x in range(4) for y in range(2)]
    return lax.ppermute(value, ("x", "y"), pairs)


def on_device(grid_embed, latent, key_weight, value_weight, out_weight, target, edges):
    out_rows = jnp.pad(out_weight, ((0, VARS_PAD - VARS), (0, 0)))
    upper_latent = band_shift(latent, -1)
    nodes1, nodes2 = ens_swap(latent, 1), ens_swap(latent, 2)
    nodes3 = ens_swap(nodes2, 1)
    halves_of_key = (key_weight[:, : D // 2], key_weight[:, D // 2 :])
    own_keys, count = call(own_kernel, [((HELD_ROWS, D), LOW), ((GROUP, GRID_DEV), F32)])(
        latent, edges, *halves_of_key
    )
    preds, share, normed_low, inverse, exps, damps, values = call(
        forward_kernel,
        [
            ((HELD, VARS_PAD, GRID_DEV), F32),
            ((PRED_ROW + VARS_PAD, GROUP), LOW),
            ((HELD, GRID_DEV, D), LOW),
            ((HELD, GRID_DEV, 128), F32),
            ((HELD, GROUPS, GROUP, GRID_DEV), LOW),
            ((HELD, GROUPS, GROUP, GRID_DEV), LOW),
            ((HELD * WINDOW, D), LOW),
        ],
        [((HELD * WINDOW, D), LOW), ((GRID_DEV, D), F32)],
    )(
        grid_embed, latent, upper_latent, *halves_of_key, value_weight, out_rows, own_keys, count
    )
    spot = (lax.axis_index("x") * 2 + lax.axis_index("y")) * ENS + lax.axis_index("ens")
    me = spot.reshape(1)
    shares = lax.all_gather(share, "ens", axis=0)
    block = (2 * HELD_ROWS, COLS)
    scalar = {0: pl.BlockSpec(memory_space=pltpu.SMEM)}
    halves, next1, next2, next3, out_grad = call(
        backward_kernel,
        [((ENS, *block), LOW), ((2 * HELD_ROWS + NEAR * SHARE, COLS), LOW)]
        + [(block, LOW)] * 2
        + [((D, VARS_PAD), LOW)],
        [((GRID_DEV, D), F32), ((VARS_PAD, GRID_DEV), F32)],
        {**scalar, 5: pl.BlockSpec((ENS, VARS_PAD, GROUP), lambda i: (0, PRED_ROW // VARS_PAD, 0))},
    )(me, grid_embed, out_rows, target, preds, shares, normed_low, inverse, exps, damps, values)
    last1, last2, last3 = (ens_swap(v, k) for k, v in ((1, next1), (2, next2), (3, next3)))
    own, upper = call(latent_kernel, [((HELD_ROWS, D), F32), ((HELD_ROWS, D), LOW)])(
        halves, key_weight, value_weight
    )
    lower = band_shift(upper, 1)
    share_block = ((FAR + 1) * SHARE, COLS)
    keep, *sends = call(
        weight_kernel,
        [(share_block, LOW)] * NEAR,
        [((D, COLS), LOW), ((NEAR * SHARE, COLS), LOW)],
        specs={
            **{i: pl.BlockSpec(memory_space=pltpu.SMEM) for i in range(1)},
            9: pl.BlockSpec((ENS, PRED_ROW, GROUP), lambda i: (0, 0, 0)),
            11: pl.BlockSpec((16, 128), lambda i: (0, 0)),
        },
    )(
        me, halves, last1, last2, last3, latent, nodes1, nodes2, nodes3, shares,
        out_grad, upper,
    )
    parts = [near_shift(value, *step) for step, value in zip(PATHS[:5], sends[:5])]
    relayed = call(relay_kernel, [(share_block, LOW), (share_block, LOW)])(
        parts[1], parts[0], sends[5], sends[6]
    )
    parts = parts[2:] + [near_shift(value, *step) for step, value in zip(PATHS[5:], relayed)]
    (total,) = call(near_sum_kernel, [((FAR, SHARE, COLS + VARS_PAD), LOW)], specs=scalar)(
        me, keep, *parts
    )
    parts = lax.all_to_all(total, "z", 0, 0, tiled=True)
    (total,) = call(sum_kernel, [((SHARE, COLS + VARS_PAD), LOW)])(parts)
    parts = [ens_swap(total, k) for k in (1, 2, 3)]
    return tuple(
        call(
            finish_kernel,
            [((16, D), F32), ((16, D), F32), ((16, VARS), F32), ((HELD, LAT_DEV, D), F32)],
            [((ENS, SHARE, COLS + VARS_PAD), LOW)],
            scalar,
        )(me, total, *parts, own, lower)
    )


def solution(mesh):
    wide = Mesh(mesh.devices.reshape(4, 8, 4, 2), ("ens", *BAND))
    in_specs = (
        P("ens", BAND, None),
        P("ens", BAND, None),
        P(),
        P(),
        P(),
        P(None, BAND),
        P(None, BAND),
    )
    out_specs = (P(BAND, None), P(BAND, None), P(BAND, None), P("ens", BAND, None))
    return jax.shard_map(
        on_device, mesh=wide, in_specs=in_specs, out_specs=out_specs, check_vma=False
    )
```
